32 devices in a mesh: groups: 2 (over x), tm: 8 (over z, y), space: 2 (over core).
Axes of the slice: x: 2, y: 2, z: 4, core: 2. Of those that a mesh axis runs over, the one named last changes fastest.
Arguments:
- latents: bfloat16 [32, 12, 80, 2240], P(('groups', 'tm'), 'space'), parts along dimension 0, may hold values from -8 to 8
- proj_weight: bfloat16 [2240, 3360], P('tm'), may hold values from -0.125 to 0.125
Outputs:
- attended: bfloat16 [32, 12, 80, 1120], P(('groups', 'tm'), 'space'), parts along dimension 0
The draws below stay inside these ranges and needn't reach their ends.
There are 2 independent parts, one for each index of `groups`. The reference program is written for one: setup_inputs(seed, part) draws one part's arguments, and reference() takes and returns one part's arrays. A program takes and returns all parts, laid end to end along the dimension named above; an argument that names none is the same for every part. Nothing has to cross between parts.
All inputs are finite; a program needn't handle non-finite values.
Results may differ from the reference program's by a relative error of at most 0.0034.
Values may be sent and summed in bfloat16 or wider, within the bound.
No kernel may reach another device: no remote copies, remote signals or barrier semaphores. Data moves between devices by JAX's collectives and lax.ppermute only.
A program may use at most 128 MiB of HBM per device.

```python
import jax
import jax.numpy as jnp
from jax import lax

D = 2240
HEADS = 10
HEAD = 112
WIDTH = 80
F_DEV = 2
FRAMES = 16
ROWS = 12


def draw_latents(key, part):
    key_scene = jax.random.fold_in(key, 11)
    key_region = jax.random.fold_in(key, 12)
    key_jitter = jax.random.fold_in(key, 13)
    scenes = jax.random.normal(key_scene, (FRAMES, 1, 1, D), jnp.float32)
    jitter = jax.random.normal(key_jitter, (FRAMES, ROWS, WIDTH, D), jnp.float32)
    region = 0.5 * jax.random.normal(key_region, (1, ROWS, 1, D), jnp.float32)
    return jnp.clip(scenes + region + jitter, -8.0, 8.0).astype(jnp.bfloat16)


def block_levels(own_key, dims, split, least, high):
    loudness = 1.0
    for position, blocks in split:
        steps = jax.random.uniform(jax.random.fold_in(jax.random.fold_in(own_key, 6), position), (blocks,), jnp.float32, least / len(split), high / len(split))
        loudness = loudness * jnp.repeat(jnp.exp(steps), dims[position] // blocks).reshape((-1,) + (1,) * (len(dims) - 1 - position))
    return loudness


def bell_draw(own_key, dims, width, reach, pieces=(), held_as=jnp.bfloat16):
    result = jax.random.normal(own_key, dims, jnp.float32) * width
    if len(pieces) > 0:
        result = block_levels(own_key, dims, pieces, -0.22, 0.18) * result
    return jnp.clip(result, min=-reach, max=reach).astype(held_as)


def setup_inputs(seed: int = 0, part: int = 0) -> dict:
    key_of = jax.random.split(jax.random.key(seed), 3)
    own_keys = jax.random.split(jax.random.fold_in(key_of[2], part), 3)
    return {
        "latents": draw_latents(jax.random.fold_in(jax.random.fold_in(key_of[2], part), 71), part),
        "proj_weight": bell_draw(key_of[1], (D, 3 * HEADS * HEAD), D ** -0.5, 0.125, ((0, 8),)),
    }


def block_states(projected_block):
    key_feats = jax.nn.relu(projected_block[:, 1]).astype(jnp.float32)
    values = projected_block[:, 2].astype(jnp.float32)
    states = jnp.einsum("nhe,nhf->hef", key_feats, values)
    key_sums = jnp.sum(key_feats, axis=0)
    return states, key_sums


def attend_block(operands):
    projected_block, states, key_sums = operands
    queries = jax.nn.relu(projected_block[:, 0]).astype(jnp.float32)
    rounded = lax.optimization_barrier(states.astype(jnp.bfloat16)).astype(jnp.float32)
    numerator = jnp.einsum("nhe,hef->nhf", queries, rounded)
    denominator = jnp.einsum("nhe,he->nh", queries, key_sums, precision=lax.Precision.HIGHEST)
    return (numerator / (denominator[:, :, None] + 1.0)).astype(jnp.bfloat16)


def reference(latents, proj_weight):
    frame_count, row_count, column_count, channels = latents.shape
    per_block = F_DEV * row_count * column_count
    block_count = frame_count // F_DEV
    tokens = latents.reshape(block_count, per_block, channels)

    def project(frame_block):
        return jnp.dot(frame_block, proj_weight, preferred_element_type=jnp.float32).astype(jnp.bfloat16)

    projected = lax.map(project, tokens).reshape(block_count, per_block, 3, HEADS, HEAD)
    states, key_sums = lax.map(block_states, projected)
    total_states = jnp.cumsum(states, axis=0)
    total_sums = jnp.cumsum(key_sums, axis=0)
    attended = lax.map(attend_block, (projected, total_states, total_sums))
    return attended.reshape(frame_count, row_count, column_count, HEADS * HEAD)
```

```python
import functools

import jax
import jax.numpy as jnp
import numpy as np
from jax import lax
from jax.experimental import pallas as pl
from jax.experimental.pallas import tpu as pltpu
from jax.sharding import PartitionSpec as P

HEADS = 10
HEAD = 112
LANES = 128
DEPTH = 256
BF = jnp.bfloat16
F32 = jnp.float32
LIMIT = 44 * 1024 * 1024


def ceil_to(value, step):
    return -(-value // step) * step


def dot(a, b):
    return jnp.dot(a, b, preferred_element_type=F32)


def params():
    return pltpu.CompilerParams(vmem_limit_bytes=LIMIT, dimension_semantics=("arbitrary",))


def cost(flops, moved):
    return pl.CostEstimate(flops=int(flops), bytes_accessed=int(moved), transcendentals=0)


def whole(shape):
    return pl.BlockSpec(shape, lambda i, *_: (0,) * len(shape))


def ring_order(count):
    if count % 2:
        return list(range(count))
    return list(range(0, count, 2)) + list(range(count - 1, 0, -2))


def slot_table(count):
    order = ring_order(count)
    up, down = count // 2, (count - 1) // 2
    table = np.zeros((count, count), np.int32)
    for at, index in enumerate(order):
        slots = [0]
        for step in range(1, up + 1):
            slots.append(-step)
            if step <= down:
                slots.append(step)
        table[index] = [order[(at + s) % count] for s in slots]
    return table


def pack_weight_kernel(meta, w_ref, p_ref, o_ref, qm_ref, qt_ref, rem_ref, *, main, heads_here):
    wide = heads_here * HEAD
    model = HEADS * HEAD
    rows = w_ref.shape[0]
    near = main // 2

    def columns(core):
        def place(ref, value, at):
            ref[:, at : at + value.shape[1]] = value

        k_at, v_at = model + core * wide, 2 * model + core * wide
        if main:
            p_rows = pl.ds(pl.multiple_of(meta[0] * near, near), near)
            o_rows = pl.ds(pl.multiple_of((1 - meta[0]) * near, near), near)
            for ref, take in ((p_ref, p_rows), (o_ref, o_rows)):
                place(ref, w_ref[take, k_at : k_at + wide], 0)
                place(ref, w_ref[take, v_at : v_at + wide], wide)
            qm_ref[...] = w_ref[core * near : (core + 1) * near, :model]
            qt_ref[...] = w_ref[(1 - core) * near : (2 - core) * near, :model]
        rem_ref[...] = jnp.zeros_like(rem_ref)
        place(rem_ref, w_ref[main:rows, k_at : k_at + wide], 0)
        place(rem_ref, w_ref[main:rows, v_at : v_at + wide], wide)
        place(rem_ref, w_ref[main:rows, :model], ceil_to(2 * wide, LANES))

    for core in range(HEADS // heads_here):
        pl.when(meta[1] == core)(functools.partial(columns, core))


def pack_weight(meta, w, main, heads_here):
    rows, wide = w.shape
    model = HEADS * HEAD
    kv = 2 * heads_here * HEAD
    near = max(main // 2, 16)
    shapes = [(near, kv), (near, kv), (near, model), (near, model)]
    shapes.append((rows - main, ceil_to(kv, LANES) + ceil_to(model, LANES)))
    return pl.pallas_call(
        functools.partial(pack_weight_kernel, main=main, heads_here=heads_here),
        grid_spec=pltpu.PrefetchScalarGridSpec(
            num_scalar_prefetch=1,
            grid=(1,),
            in_specs=[whole(w.shape)],
            out_specs=[whole(s) for s in shapes],
        ),
        out_shape=[jax.ShapeDtypeStruct(s, BF) for s in shapes],
        compiler_params=params(),
        cost_estimate=cost(0, 2 * w.size * 2),
        name="pack_weight",
    )(meta, w)


def pack_tokens_kernel(x_ref, o_ref, *, rows, main, count):
    rest = rows - main
    if main:
        for j in range(count):
            o_ref[:, j * main : (j + 1) * main] = x_ref[:, j * rows : j * rows + main]
    if rest:
        at = count * main
        pieces = [x_ref[:, j * rows + main : (j + 1) * rows] for j in range(count)]
        o_ref[:, at : at + count * rest] = jnp.concatenate(pieces, axis=1)


def pack_tokens(x, rows, main, count, block):
    if main == 0:
        return x
    tokens, channels = x.shape
    spec = pl.BlockSpec((block, channels), lambda i: (i, 0))
    return pl.pallas_call(
        functools.partial(pack_tokens_kernel, rows=rows, main=main, count=count),
        grid=(tokens // block,),
        in_specs=[spec],
        out_specs=spec,
        out_shape=jax.ShapeDtypeStruct(x.shape, BF),
        compiler_params=params(),
        cost_estimate=cost(0, 4 * x.size),
        name="pack_tokens",
    )(x)


def fill(weights, meta, which, pieces, main):
    near = main // 2
    first = meta[which]
    for s in range(len(pieces) // 2):
        at = pl.multiple_of(s * main + first * near, near)
        weights[pl.ds(at, near), :] = pieces[2 * s][...]
        at = pl.multiple_of(s * main + (1 - first) * near, near)
        weights[pl.ds(at, near), :] = pieces[2 * s + 1][...]


def project(meta, slots, x_ref, weights, main):
    taken = []
    for s in slots:
        at = pl.multiple_of(meta[2 + s] * main, main)
        taken.append(x_ref[:, pl.ds(at, main)])
    x = taken[0] if len(taken) == 1 else jnp.concatenate(taken, axis=1)
    return dot(x, weights[...])


def early_kernel(meta, x_ref, *refs, slots, main, which):
    pieces, out_ref, weights = refs[:-2], refs[-2], refs[-1]

    @pl.when(pl.program_id(0) == 0)
    def _():
        fill(weights, meta, which, pieces, main)

    out_ref[...] = project(meta, slots, x_ref, weights, main)


def early(meta, x, pieces, slots, main, which, block, name):
    tokens, channels = x.shape
    wide = pieces[0].shape[1]
    return pl.pallas_call(
        functools.partial(early_kernel, slots=slots, main=main, which=which),
        grid_spec=pltpu.PrefetchScalarGridSpec(
            num_scalar_prefetch=1,
            grid=(tokens // block,),
            in_specs=[pl.BlockSpec((block, channels), lambda i, *_: (i, 0))]
            + [whole(p.shape) for p in pieces],
            out_specs=pl.BlockSpec((block, wide), lambda i, *_: (i, 0)),
            scratch_shapes=[pltpu.VMEM((len(slots) * main, wide), BF)],
        ),
        out_shape=jax.ShapeDtypeStruct((tokens, wide), F32),
        compiler_params=params(),
        cost_estimate=cost(2 * tokens * len(slots) * main * wide, tokens * (channels * 2 + wide * 4)),
        name=name,
    )(meta, x, *pieces)


def projected_block(meta, x_ref, rem_ref, acc_ref, weights, slots, main, rest, wide):
    count_main = x_ref.shape[1] - rest
    total = dot(x_ref[:, count_main:], rem_ref[:, :wide])
    if slots:
        total = total + project(meta, slots, x_ref, weights, main)
    if acc_ref is not None:
        total = total + acc_ref[...]
    return total.astype(BF)


def states_kernel(meta, x_ref, rem_ref, prior_ref, *refs, slots, main, rest, has_acc, heads_here):
    acc_ref = refs[0] if has_acc else None
    pieces = refs[has_acc : has_acc + 2 * len(slots)]
    out_ref, weights, values, total = refs[has_acc + 2 * len(slots) :]
    wide = heads_here * HEAD
    step = pl.program_id(0)

    @pl.when(step == 0)
    def _():
        if slots:
            fill(weights, meta, 0, pieces, main)
        values[...] = jnp.ones_like(values)
        total[...] = jnp.zeros_like(total)

    projected = projected_block(meta, x_ref, rem_ref, acc_ref, weights, slots, main, rest, 2 * wide)
    feats = jnp.maximum(projected[:, :wide], 0)
    values[:, :wide] = projected[:, wide:]
    total[...] += lax.dot_general(
        feats, values[...], (((0,), (0,)), ((), ())), preferred_element_type=F32
    )

    @pl.when(step == pl.num_programs(0) - 1)
    def _():
        sums = total[:, wide : wide + LANES - HEAD]
        for h in range(heads_here):
            rows = slice(h * HEAD, (h + 1) * HEAD)
            out_ref[rows, :HEAD] = total[rows, rows] + prior_ref[rows, :HEAD]
        out_ref[:, HEAD:] = sums + prior_ref[:, HEAD:]


def block_states(meta, x, rem, prior, acc, pieces, slots, main, rest, heads_here, block):
    tokens, channels = x.shape
    wide = heads_here * HEAD
    kv = 2 * wide
    room = ceil_to(wide + LANES, 256)
    given = ([acc] if acc is not None else []) + list(pieces)
    specs = [pl.BlockSpec((block, kv), lambda i, *_: (i, 0))] if acc is not None else []
    specs += [whole(p.shape) for p in pieces]
    depth = len(slots) * main + rest
    return pl.pallas_call(
        functools.partial(
            states_kernel,
            slots=slots,
            main=main,
            rest=rest,
            has_acc=int(acc is not None),
            heads_here=heads_here,
        ),
        grid_spec=pltpu.PrefetchScalarGridSpec(
            num_scalar_prefetch=1,
            grid=(tokens // block,),
            in_specs=[
                pl.BlockSpec((block, channels), lambda i, *_: (i, 0)),
                whole((rem.shape[0], ceil_to(kv, LANES))),
                whole(prior.shape),
            ]
            + specs,
            out_specs=whole((wide, LANES)),
            scratch_shapes=[
                pltpu.VMEM((max(len(slots) * main, 16), kv), BF),
                pltpu.VMEM((block, room), BF),
                pltpu.VMEM((wide, room), F32),
            ],
        ),
        out_shape=jax.ShapeDtypeStruct((wide, LANES), F32),
        compiler_params=params(),
        cost_estimate=cost(2 * tokens * (depth * kv + wide * room), tokens * (channels * 2 + kv * 4)),
        name="states",
    )(meta, x, rem, prior, *given)


def bands():
    model = HEADS * HEAD
    found = []
    for left in range(0, model, 256):
        right = min(left + 256, model)
        heads = range(left // HEAD, -(-right // HEAD))
        low = heads[0] * HEAD // LANES * LANES
        high = min(ceil_to((heads[-1] + 1) * HEAD, LANES), model)
        found.append((left, right, low, high, heads))
    return found


def expand_kernel(meta, mine_ref, theirs_ref, s_ref, hi_ref, lo_ref, *, heads_here):
    for ref in (s_ref, hi_ref, lo_ref):
        ref[...] = jnp.zeros_like(ref)
    halves = []
    for half in range(HEADS // heads_here):
        halves.append(jnp.where(meta[1] == half, mine_ref[...], theirs_ref[...]))
    base = 0
    for left, right, low, high, heads in bands():
        for h in heads:
            block = halves[h // heads_here]
            at = (h % heads_here) * HEAD
            states = block[at : at + HEAD, :HEAD]
            sums = jnp.broadcast_to(block[at : at + HEAD, HEAD : HEAD + 1], (HEAD, HEAD))
            high_part = sums.astype(BF)
            low_part = (sums - high_part.astype(F32)).astype(BF)
            begin, end = max(h * HEAD, left), min((h + 1) * HEAD, right)
            rows = slice(base + h * HEAD - low, base + (h + 1) * HEAD - low)
            cols = slice(begin - left, end - left)
            take = slice(begin - h * HEAD, end - h * HEAD)
            s_ref[rows, cols] = states[:, take].astype(BF)
            hi_ref[rows, cols] = high_part[:, take]
            lo_ref[rows, cols] = low_part[:, take]
        base += high - low


def expand(meta, mine, theirs, heads_here):
    rows = sum(high - low for _, _, low, high, _ in bands())
    shape = (rows, 256)
    return pl.pallas_call(
        functools.partial(expand_kernel, heads_here=heads_here),
        grid_spec=pltpu.PrefetchScalarGridSpec(
            num_scalar_prefetch=1,
            grid=(1,),
            in_specs=[whole(mine.shape), whole(theirs.shape)],
            out_specs=[whole(shape)] * 3,
        ),
        out_shape=[jax.ShapeDtypeStruct(shape, BF)] * 3,
        compiler_params=params(),
        cost_estimate=cost(0, 6 * rows * 256),
        name="expand",
    )(meta, mine, theirs)


def attend_kernel(meta, x_ref, rem_ref, s_ref, hi_ref, lo_ref, *refs, slots, main, rest, has_acc):
    acc_ref = refs[0] if has_acc else None
    pieces = refs[has_acc : has_acc + 2 * len(slots)]
    out_ref, weights, queries = refs[has_acc + 2 * len(slots) :]
    model = HEADS * HEAD

    @pl.when(pl.program_id(0) == 0)
    def _():
        if slots:
            fill(weights, meta, 1, pieces, main)

    projected = projected_block(meta, x_ref, rem_ref, acc_ref, weights, slots, main, rest, model)
    queries[...] = jnp.maximum(projected, 0)
    base = 0
    for left, right, low, high, _ in bands():
        rows = slice(base, base + high - low)
        q = queries[:, low:high]
        numerator = dot(q, s_ref[rows, :])
        denominator = dot(q, hi_ref[rows, :]) + dot(q, lo_ref[rows, :]) + 1.0
        out_ref[:, left:right] = (numerator / denominator).astype(BF)[:, : right - left]
        base += high - low


def attend(meta, x, rem, banded, acc, pieces, slots, main, rest, kv_wide, block):
    tokens, channels = x.shape
    model = HEADS * HEAD
    room = ceil_to(model, LANES)
    given = ([acc] if acc is not None else []) + list(pieces)
    specs = [pl.BlockSpec((block, model), lambda i, *_: (i, 0))] if acc is not None else []
    specs += [whole(p.shape) for p in pieces]
    depth = len(slots) * main + rest
    return pl.pallas_call(
        functools.partial(
            attend_kernel, slots=slots, main=main, rest=rest, has_acc=int(acc is not None)
        ),
        grid_spec=pltpu.PrefetchScalarGridSpec(
            num_scalar_prefetch=1,
            grid=(tokens // block,),
            in_specs=[
                pl.BlockSpec((block, channels), lambda i, *_: (i, 0)),
                pl.BlockSpec((rem.shape[0], room), lambda i, *_: (0, ceil_to(kv_wide, LANES) // room)),
            ]
            + [whole(b.shape) for b in banded]
            + specs,
            out_specs=pl.BlockSpec((block, model), lambda i, *_: (i, 0)),
            scratch_shapes=[
                pltpu.VMEM((max(len(slots) * main, 16), model), BF),
                pltpu.VMEM((block, model), BF),
            ],
        ),
        out_shape=jax.ShapeDtypeStruct((tokens, model), BF),
        compiler_params=params(),
        cost_estimate=cost(2 * tokens * model * (depth + 1500), tokens * (channels * 2 + model * 6)),
        name="attend",
    )(meta, x, rem, *banded, *given)


def swap_pairs(count):
    return [(i, i ^ 1) for i in range(count)]


def ring_steps(count):
    order = ring_order(count)
    forward = [(order[i], order[(i + 1) % count]) for i in range(count)]
    return forward, [(b, a) for a, b in forward]


def gather_columns(near, other, count, groups):
    forward, backward = ring_steps(count)
    slots = [(near, other)]
    up_near = down_near = near
    up_other = down_other = other
    for step in range(1, count // 2 + 1):
        down_here = step <= (count - 1) // 2
        up_near = lax.ppermute(up_near, "tm", forward)
        if down_here:
            down_near = lax.ppermute(down_near, "tm", backward)
        if step <= 1:
            up_other = lax.ppermute(up_other, "tm", forward)
        else:
            up_other = lax.ppermute(up_near, "groups", swap_pairs(groups))
        slots.append((up_near, up_other))
        if down_here:
            if step <= 2:
                down_other = lax.ppermute(down_other, "tm", backward)
            else:
                down_other = lax.ppermute(down_near, "groups", swap_pairs(groups))
            slots.append((down_near, down_other))
    return slots


def gather_queries(mine, theirs, count):
    forward, backward = ring_steps(count)
    slots = [(mine, theirs)]
    up = down = mine
    for step in range(1, count // 2 + 1):
        up = lax.ppermute(up, "tm", forward)
        slots.append((up, lax.ppermute(up, "space", swap_pairs(2))))
        if step <= (count - 1) // 2:
            down = lax.ppermute(down, "tm", backward)
            slots.append((down, lax.ppermute(down, "space", swap_pairs(2))))
    return slots


def running_total(value, count):
    reach = 1
    while reach < count:
        pairs = [(i, i + reach) for i in range(count - reach)]
        value = value + lax.ppermute(value, "tm", pairs)
        reach *= 2
    return value


def flat(slots):
    return [part for slot in slots for part in slot]


def on_device(latents, proj_weight):
    frame_count, band_rows, column_count, channels = latents.shape
    rows = proj_weight.shape[0]
    count = lax.axis_size("tm")
    groups = lax.axis_size("groups")
    bands_here = lax.axis_size("space")
    heads_here = HEADS // bands_here
    kv_wide = 2 * heads_here * HEAD
    main = DEPTH if rows >= DEPTH and groups % 2 == 0 else 0
    rest = (rows - main) * count
    tokens = frame_count * band_rows * column_count
    block = 240 if tokens % 240 == 0 else tokens

    here = jnp.asarray(slot_table(count))[lax.axis_index("tm")]
    plane = lax.rem(lax.axis_index("groups"), 2)
    meta = jnp.concatenate([jnp.stack([plane, lax.axis_index("space")]), here]).astype(jnp.int32)

    near, other, q_mine, q_theirs, left_over = pack_weight(meta, proj_weight, main, heads_here)
    rem = lax.all_gather(left_over, "tm", axis=0, tiled=True)
    x = pack_tokens(latents.reshape(tokens, channels), rows, main, count, block)
    x_other = lax.ppermute(x, "space", swap_pairs(bands_here))

    prior = jnp.zeros((heads_here * HEAD, LANES), F32)
    if main:
        kv = gather_columns(near, other, count, groups)
        queries = gather_queries(q_mine, q_theirs, count)
        cut = (5 * count) // 8
        first, last = tuple(range(cut)), tuple(range(cut, count))
        kv_acc = [early(meta, t, flat(kv[:cut]), first, main, 0, block, "kv_early") for t in (x, x_other)]
        q_acc = early(meta, x, flat(queries[:cut]), first, main, 1, block, "q_early")
        kv_late, q_late = flat(kv[cut:]), flat(queries[cut:])
    else:
        kv_acc, q_acc, kv_late, q_late, last = [None, None], None, [], [], ()
    for tok, acc in zip((x, x_other), kv_acc):
        prior = block_states(meta, tok, rem, prior, acc, kv_late, last, main, rest, heads_here, block)
    total = running_total(prior, count)
    total_other = lax.ppermute(total, "space", swap_pairs(bands_here))
    banded = expand(meta, total, total_other, heads_here)
    out = attend(meta, x, rem, banded, q_acc, q_late, last, main, rest, kv_wide, block)
    return out.reshape(frame_count, band_rows, column_count, HEADS * HEAD)


def solution(mesh):
    return jax.shard_map(
        on_device,
        mesh=mesh,
        in_specs=(P(("groups", "tm"), "space", None, None), P("tm", None)),
        out_specs=P(("groups", "tm"), "space", None, None),
        check_vma=False,
    )
```

```python
import functools

import jax
import jax.numpy as jnp
import numpy as np
from jax import lax
from jax.experimental import pallas as pl
from jax.experimental.pallas import tpu as pltpu
from jax.sharding import PartitionSpec as P

HEADS = 10
HEAD = 112
LANES = 128
DEPTH = 256
BF = jnp.bfloat16
F32 = jnp.float32
LIMIT = 16 * 1024 * 1024


def ceil_to(value, step):
    return -(-value // step) * step


def dot(a, b):
    return jnp.dot(a, b, preferred_element_type=F32)


def params():
    return pltpu.CompilerParams(vmem_limit_bytes=LIMIT, dimension_semantics=("arbitrary",))


def cost(flops, moved):
    return pl.CostEstimate(flops=int(flops), bytes_accessed=int(moved), transcendentals=0)


def whole(shape):
    return pl.BlockSpec(shape, lambda i, *_: (0,) * len(shape))


def ring_order(count):
    if count % 2:
        return list(range(count))
    return list(range(0, count, 2)) + list(range(count - 1, 0, -2))


def slot_table(count):
    order = ring_order(count)
    up, down = count // 2, (count - 1) // 2
    table = np.zeros((count, count), np.int32)
    for at, index in enumerate(order):
        slots = [0]
        for step in range(1, up + 1):
            slots.append(-step)
            if step <= down:
                slots.append(step)
        table[index] = [order[(at + s) % count] for s in slots]
    return table


def split_rows(rows):
    third = ceil_to(DEPTH // 3, 16)
    spare = ceil_to((rows - DEPTH + 1) // 2, 16)
    return third, DEPTH - 2 * third, spare


def resident(kernel, meta, operands, outs, scratch, flops, name, aliases=None):
    in_vmem = pl.BlockSpec(memory_space=pltpu.VMEM)
    return pl.pallas_call(
        kernel,
        in_specs=[pl.BlockSpec(memory_space=pltpu.SMEM)] + [in_vmem] * len(operands),
        out_specs=[in_vmem] * len(outs),
        out_shape=outs,
        scratch_shapes=scratch,
        input_output_aliases=aliases or {},
        compiler_params=pltpu.CompilerParams(vmem_limit_bytes=LIMIT),
        cost_estimate=cost(flops, 0),
        name=name,
    )(meta, *operands)


def key_value_columns(meta, heads_here, run):
    wide, model = heads_here * HEAD, HEADS * HEAD

    def on_core(core):
        for part in (1, 2):
            begin = part * model + core * wide
            run(slice(begin, begin + wide), slice((part - 1) * wide, part * wide))

    for core in range(HEADS // heads_here):
        pl.when(meta[1] == core)(functools.partial(on_core, core))


def pack_first_kernel(meta, w_ref, out_ref, *, heads_here):
    rows = w_ref.shape[0]
    third, shared, _ = split_rows(rows)
    own_rows = pl.ds(pl.multiple_of(meta[0] * third, 16), third)
    filled = third + shared + rows - DEPTH
    out_ref[third + shared :, :] = jnp.zeros((out_ref.shape[0] - third - shared, out_ref.shape[1]), BF)

    def run(of, to):
        out_ref[:third, to] = w_ref[own_rows, of]
        out_ref[third : third + shared, to] = w_ref[2 * third : DEPTH, of]
        out_ref[third + shared : filled, to] = w_ref[DEPTH:, of]

    key_value_columns(meta, heads_here, run)


def pack_rest_kernel(meta, w_ref, after_ref, other_ref, mine_ref, theirs_ref, *, heads_here):
    rows = w_ref.shape[0]
    third, _, spare = split_rows(rows)
    half, model = DEPTH // 2, HEADS * HEAD
    other_rows = pl.ds(pl.multiple_of((1 - meta[0]) * third, 16), third)

    def run(of, to):
        other_ref[:, to] = w_ref[other_rows, of]

    key_value_columns(meta, heads_here, run)

    def queries(out_ref, core):
        out_ref[:half, :] = w_ref[core * half : (core + 1) * half, :model]
        out_ref[half:, :] = jnp.zeros((spare, model), BF)
        begin = DEPTH + core * spare
        count = min(spare, rows - begin)
        out_ref[half : half + count, :] = w_ref[begin : begin + count, :model]

    for core in range(2):
        pl.when(meta[1] == core)(functools.partial(queries, mine_ref, core))
        pl.when(meta[1] == 1 - core)(functools.partial(queries, theirs_ref, core))


def pack_first(meta, w, heads_here):
    third, shared, spare = split_rows(w.shape[0])
    wide = 2 * heads_here * HEAD
    out = jax.ShapeDtypeStruct((third + shared + 2 * spare, wide), BF)
    kernel = functools.partial(pack_first_kernel, heads_here=heads_here)
    return resident(kernel, meta, [w], [out], [], 1e9, "pack_first")[0]


def pack_rest(meta, w, after, heads_here):
    third, _, spare = split_rows(w.shape[0])
    half = DEPTH // 2 + spare
    outs = [jax.ShapeDtypeStruct((third, 2 * heads_here * HEAD), BF)]
    outs += [jax.ShapeDtypeStruct((half, HEADS * HEAD), BF)] * 2
    kernel = functools.partial(pack_rest_kernel, heads_here=heads_here)
    return resident(kernel, meta, [w, after], outs, [], 1e9, "pack_rest")


def pack_tokens_kernel(x_ref, after_ref, o_ref, *, rows, count):
    spare = split_rows(rows)[2]
    rest = rows - DEPTH
    blank = jnp.zeros((x_ref.shape[0], 2 * spare - rest), x_ref.dtype)
    left_over = []
    for j in range(count):
        at = j * rows
        o_ref[:, j * DEPTH : (j + 1) * DEPTH] = x_ref[:, at : at + DEPTH]
        left_over += [x_ref[:, at + DEPTH : at + rows], blank]
    o_ref[:, count * DEPTH :] = jnp.concatenate(left_over, axis=1)


def pack_tokens(x, after, rows, count, block):
    tokens, channels = x.shape
    depth = count * (DEPTH + 2 * split_rows(rows)[2])
    return pl.pallas_call(
        functools.partial(pack_tokens_kernel, rows=rows, count=count),
        grid=(tokens // block,),
        in_specs=[
            pl.BlockSpec((block, channels), lambda i: (i, 0)),
            pl.BlockSpec(memory_space=pl.ANY),
        ],
        out_specs=pl.BlockSpec((block, depth), lambda i: (i, 0)),
        out_shape=jax.ShapeDtypeStruct((tokens, depth), BF),
        compiler_params=params(),
        cost_estimate=cost(0, 4 * x.size),
        name="pack_tokens",
    )(x, after)


def put(weights, at, step, value):
    weights[pl.ds(pl.multiple_of(at, step), value.shape[0]), :] = value


def fill_keys_values(weights, meta, slots, pieces, rows):
    third, shared, spare = split_rows(rows)
    for s in range(len(slots)):
        own, other, common = pieces[3 * s : 3 * s + 3]
        put(weights, s * DEPTH + meta[0] * third, 16, own[:third, :])
        put(weights, s * DEPTH + (1 - meta[0]) * third, 16, other[...])
        at = common.shape[0] - shared - 2 * spare
        weights[s * DEPTH + 2 * third : (s + 1) * DEPTH, :] = common[at : at + shared, :]


def fill_queries(weights, meta, slots, pieces, rows):
    half = DEPTH // 2
    for s in range(len(slots)):
        mine, theirs = pieces[2 * s : 2 * s + 2]
        put(weights, s * DEPTH + meta[1] * half, 16, mine[:half, :])
        put(weights, s * DEPTH + (1 - meta[1]) * half, 16, theirs[:half, :])


def fill_left_over(weights, meta, base, pieces, rows, of_keys):
    spare = split_rows(rows)[2]
    if of_keys:
        for s, common in enumerate(pieces):
            put(weights, base + meta[2 + s] * 2 * spare, 16, common[common.shape[0] - 2 * spare :, :])
        return
    for s in range(len(pieces) // 2):
        at = base + meta[2 + s] * 2 * spare
        put(weights, at + meta[1] * spare, 16, pieces[2 * s][DEPTH // 2 :, :])
        put(weights, at + (1 - meta[1]) * spare, 16, pieces[2 * s + 1][DEPTH // 2 :, :])


def token_columns(x_ref, rows, meta, slots, count, with_rest):
    taken = [x_ref[rows, pl.ds(pl.multiple_of(meta[2 + s] * DEPTH, DEPTH), DEPTH)] for s in slots]
    if with_rest:
        taken.append(x_ref[rows, count * DEPTH :])
    return jnp.concatenate(taken, axis=1)


def every_block(xs, block, run):
    tokens = xs[0].shape[0]
    for band, x_ref in enumerate(xs):

        def step(i, carry, band=band, x_ref=x_ref):
            at = pl.multiple_of(i * block, block)
            run(x_ref, pl.ds(at, block), pl.ds(pl.multiple_of(at + band * tokens, block), block))
            return carry

        lax.fori_loop(0, tokens // block, step, 0)


def project_kernel(meta, *refs, plan, finish):
    bands_in, slots, count, rows, of_keys, has_acc, with_rest, block = plan
    xs, refs = refs[:bands_in], refs[bands_in:]
    acc_ref, refs = (refs[0], refs[1:]) if has_acc else (None, refs)
    many = (3 if of_keys else 2) * len(slots)
    pieces, refs = refs[:many], refs[many:]
    lasts = (1 if of_keys else 2) * count if with_rest else 0
    rest_pieces, refs = refs[:lasts], refs[lasts:]
    weights, refs = refs[-1], refs[:-1]
    (fill_keys_values if of_keys else fill_queries)(weights, meta, slots, pieces, rows)
    if with_rest:
        fill_left_over(weights, meta, len(slots) * DEPTH, rest_pieces, rows, of_keys)

    def run(x_ref, rows_here, rows_of_all):
        x = token_columns(x_ref, rows_here, meta, slots, count, with_rest)
        total = dot(x, weights[...])
        if has_acc:
            total = total + acc_ref[rows_of_all, :]
        finish(refs, total, rows_of_all)

    every_block(xs, block, run)


def keep(refs, total, rows):
    refs[0][rows, :] = total


def keep_features(refs, total, rows):
    refs[0][rows, :] = jnp.maximum(total.astype(BF), 0)


def project(meta, xs, acc, pieces, rest_pieces, plan, finish, outs, scratch, more_flops, name):
    bands_in, slots, count, rows, of_keys, has_acc, with_rest, block = plan
    wide = pieces[0].shape[1]
    depth = len(slots) * DEPTH + with_rest * count * 2 * split_rows(rows)[2]
    tokens = bands_in * xs[0].shape[0]
    operands = [*xs, *([acc] if has_acc else []), *pieces, *rest_pieces]
    return resident(
        functools.partial(project_kernel, plan=plan, finish=finish),
        meta,
        operands,
        outs,
        [*scratch, pltpu.VMEM((depth, wide), BF)],
        2 * tokens * depth * wide + more_flops,
        name,
        {1 + bands_in: 0} if has_acc and outs[0].shape == acc.shape and outs[0].dtype == acc.dtype else None,
    )[0]


def states_kernel(meta, *refs, plan, heads_here):
    out_ref, values, total, weights = refs[-4:]
    wide = heads_here * HEAD
    values[...] = jnp.ones_like(values)
    total[...] = jnp.zeros_like(total)

    def finish(_, projected, rows):
        projected = projected.astype(BF)
        feats = jnp.maximum(projected[:, :wide], 0)
        values[:, :wide] = projected[:, wide:]
        total[...] += lax.dot_general(
            feats, values[...], (((0,), (0,)), ((), ())), preferred_element_type=F32
        )

    project_kernel(meta, *refs, plan=plan, finish=finish)
    for h in range(heads_here):
        rows = slice(h * HEAD, (h + 1) * HEAD)
        out_ref[rows, :HEAD] = total[rows, rows]
    out_ref[:, HEAD:] = total[:, wide : wide + LANES - HEAD]


def block_states(meta, xs, acc, pieces, rest_pieces, plan, heads_here):
    wide = heads_here * HEAD
    room = ceil_to(wide + LANES, 256)
    bands_in, slots, count, rows, _, has_acc, with_rest, block = plan
    depth = len(slots) * DEPTH + with_rest * count * 2 * split_rows(rows)[2]
    tokens = bands_in * xs[0].shape[0]
    operands = [*xs, acc, *pieces, *rest_pieces]
    return resident(
        functools.partial(states_kernel, plan=plan, heads_here=heads_here),
        meta,
        operands,
        [jax.ShapeDtypeStruct((wide, LANES), F32)],
        [
            pltpu.VMEM((block, room), BF),
            pltpu.VMEM((wide, room), F32),
            pltpu.VMEM((depth, 2 * wide), BF),
        ],
        2 * tokens * (depth * 2 * wide + wide * room),
        "states",
    )[0]


def bands():
    model = HEADS * HEAD
    found = []
    for left in range(0, model, 256):
        right = min(left + 256, model)
        heads = range(left // HEAD, -(-right // HEAD))
        low = heads[0] * HEAD // LANES * LANES
        high = min(ceil_to((heads[-1] + 1) * HEAD, LANES), model)
        found.append((left, right, low, high, heads))
    return found


def attend_kernel(meta, q_ref, mine_ref, theirs_ref, out_ref, states, sums, spread, *, heads_here):
    @pl.when(pl.program_id(0) == 0)
    def _():
        states[...] = jnp.zeros_like(states)
        sums[...] = jnp.zeros_like(sums)
        mine, theirs = mine_ref[...], theirs_ref[...]
        parts = [jnp.where(meta[1] == k, mine, theirs) for k in range(HEADS // heads_here)]
        base = 0
        for left, right, low, high, heads in bands():
            for h in heads:
                at = (h % heads_here) * HEAD
                begin, end = max(h * HEAD, left), min((h + 1) * HEAD, right)
                rows = slice(base + h * HEAD - low, base + (h + 1) * HEAD - low)
                block = parts[h // heads_here][at : at + HEAD, begin - h * HEAD : end - h * HEAD]
                states[rows, begin - left : end - left] = block.astype(BF)
            base += high - low
        lane = lax.broadcasted_iota(jnp.int32, (HEAD, LANES), 1)
        for h in range(HEADS):
            at = (h % heads_here) * HEAD
            key_sums = parts[h // heads_here][at : at + HEAD, HEAD : HEAD + 1]
            key_sums = jnp.broadcast_to(key_sums, (HEAD, LANES))
            upper = key_sums.astype(BF).astype(F32)
            chosen = jnp.where(lane == h, upper, jnp.where(lane == h + 64, key_sums - upper, 0.0))
            sums[h * HEAD : (h + 1) * HEAD, :] = chosen.astype(BF)
        head = lax.broadcasted_iota(jnp.int32, spread.shape, 0) % 64 * HEAD
        column = lax.broadcasted_iota(jnp.int32, spread.shape, 1)
        spread[...] = jnp.where((column >= head) & (column < head + HEAD), 1.0, 0.0).astype(BF)

    rows_here = pl.ds(pl.multiple_of(pl.program_id(0) * out_ref.shape[0], 16), out_ref.shape[0])
    total = dot(q_ref[rows_here, :], sums[...])
    low_lane = lax.broadcasted_iota(jnp.int32, total.shape, 1) >= 64
    denominator = total + pltpu.roll(total, 64, 1) + 1.0
    share = 1.0 / denominator
    upper = share.astype(BF).astype(F32)
    share = jnp.where(low_lane, share - upper, upper).astype(BF)
    base = 0
    for left, right, low, high, _ in bands():
        numerator = dot(q_ref[rows_here, low:high], states[base : base + high - low, :])
        scale = dot(share, spread[:, left : left + 256])
        out_ref[:, left:right] = (numerator * scale).astype(BF)[:, : right - left]
        base += high - low


def attend(meta, queries, mine, theirs, heads_here, block):
    tokens, model = queries.shape
    rows = sum(high - low for _, _, low, high, _ in bands())
    spec = pl.BlockSpec((block, model), lambda i, *_: (i, 0))
    return pl.pallas_call(
        functools.partial(attend_kernel, heads_here=heads_here),
        grid_spec=pltpu.PrefetchScalarGridSpec(
            num_scalar_prefetch=1,
            grid=(tokens // block,),
            in_specs=[pl.BlockSpec(memory_space=pltpu.VMEM)] * 3,
            out_specs=spec,
            scratch_shapes=[
                pltpu.VMEM((rows, 256), BF),
                pltpu.VMEM((model, LANES), BF),
                pltpu.VMEM((LANES, ceil_to(model, 256)), BF),
            ],
        ),
        out_shape=jax.ShapeDtypeStruct((tokens, model), BF),
        compiler_params=params(),
        cost_estimate=cost(2 * tokens * model * 800, tokens * model * 4),
        name="attend",
    )(meta, queries, mine, theirs)


def swap_pairs(count):
    return [(i, i ^ 1) for i in range(count)]


def ring_steps(count):
    order = ring_order(count)
    forward = [(order[i], order[(i + 1) % count]) for i in range(count)]
    return forward, [(b, a) for a, b in forward]


def running_total(states, sums, count, alongside=None):
    reach, hop = 1, 0
    wide, room = states.shape[-1], sums.shape[-1]
    while reach < count:
        pairs = [(i, i + reach) for i in range(count - reach)]
        upper = sums.astype(BF)
        lower = (sums - upper.astype(F32)).astype(BF)
        sent = jnp.concatenate([states.astype(BF), upper, lower], axis=-1)
        got = lax.ppermute(sent, "tm", pairs)
        if alongside is not None:
            got = alongside(hop, got)
        got = got.astype(F32)
        states = states + got[..., :wide]
        sums = sums + (got[..., wide : wide + room] + got[..., wide + room :])
        reach, hop = reach * 2, hop + 1
    return states, sums


def tie(*values):
    return lax.optimization_barrier(values)


def ring_form(latents, proj_weight):
    frame_count, band_rows, column_count, channels = latents.shape
    rows = proj_weight.shape[0]
    third = split_rows(rows)[0]
    count, groups = lax.axis_size("tm"), lax.axis_size("groups")
    heads_here = HEADS // 2
    tokens = frame_count * band_rows * column_count
    block = 480 if tokens % 480 == 0 else tokens

    forward, backward = ring_steps(count)
    across, over = swap_pairs(groups), swap_pairs(2)
    up_last, down_last = count // 2, (count - 1) // 2

    def ring(value, up):
        return lax.ppermute(value, "tm", forward if up else backward)

    def plane_swap(value):
        return lax.ppermute(value[:third], "groups", across)

    def core_swap(value):
        return lax.ppermute(value, "space", over)

    here = jnp.asarray(slot_table(count))[lax.axis_index("tm")]
    plane = lax.rem(lax.axis_index("groups"), 2)
    meta = jnp.concatenate([jnp.stack([plane, lax.axis_index("space")]), here]).astype(jnp.int32)

    own = pack_first(meta, proj_weight, heads_here)
    other, mine, theirs = pack_rest(meta, proj_weight, own, heads_here)
    x = pack_tokens(latents.reshape(tokens, channels), mine, rows, count, block)

    queries_up, queries_down = [mine], [mine]

    def next_queries():
        if len(queries_up) <= up_last - (up_last > down_last):
            queries_up.append(ring(queries_up[-1], True))
        if len(queries_down) <= up_last:
            queries_down.append(ring(queries_down[-1], False))

    def with_queries(*values):
        *values, queries_up[-1], queries_down[-1] = tie(*values, queries_up[-1], queries_down[-1])
        next_queries()
        return values

    def plan(bands_in, which, of_keys, has_acc, with_rest):
        return (bands_in, tuple(which), count, rows, of_keys, has_acc, with_rest, block)

    kv_shape = jax.ShapeDtypeStruct((2 * tokens, 2 * heads_here * HEAD), F32)

    def add_keys_values(acc, which):
        pieces = [part for s in which for part in slots[s]]
        settings = plan(2, which, True, acc is not None, False)
        return project(meta, both, acc, pieces, [], settings, keep, [kv_shape], [], 0, "kv_part")

    slots = [[own, other, own]]
    up = down = own
    swapping, acc = [], None
    for step in range(1, up_last + 1):
        full = step <= down_last
        up = ring(up if full else up[:third], True)
        down = ring(down if full else down[third:], False)
        if step == 1:
            x = tie(x, up, down)[0]
            x_other = core_swap(x)
            both = (x, x_other)
        elif step == up_last:
            acc = add_keys_values(None, range(len(slots) - 2))
            acc, up, down, *swapping = with_queries(acc, up, down, *swapping)
        else:
            x_other, up, down, *swapping = tie(x_other, up, down, *swapping)
            both = (x, x_other)
        if swapping:
            slots[-2][1], slots[-1][1] = swapping
        swapping = [plane_swap(up)] + ([plane_swap(down)] if full else [])
        if full:
            slots += [[up, swapping[0], up], [down, swapping[1], down]]
        else:
            slots += [[up, swapping[0], down]]
        if step + 1 == up_last:
            next_queries()
    final = range(len(slots) - len(swapping), len(slots))
    acc = add_keys_values(acc, range(final[0] - 2, final[0]))
    acc, *swapping = with_queries(acc, *swapping)
    for s, value in zip(final, swapping):
        slots[s][1] = value

    pieces = [part for s in final for part in slots[s]]
    commons = [slot[2] for slot in slots]
    payload = block_states(meta, both, acc, pieces, commons, plan(2, final, True, True, True), heads_here)
    (payload,) = with_queries(payload)

    found = [[mine, theirs]]
    cut = (5 * count) // 8

    def query_slots(step):
        for way in (queries_up, queries_down):
            if step < len(way):
                found.append([way[step], core_swap(way[step])])

    def project_queries(acc, which, finish, dtype, name):
        last = which[-1] == count - 1
        pieces = [part for s in which for part in found[s]]
        every = [part for s in found for part in s] if last else []
        settings = plan(1, which, False, acc is not None, last)
        out = jax.ShapeDtypeStruct((tokens, HEADS * HEAD), dtype)
        return project(meta, (x,), acc, pieces, every, settings, finish, [out], [], 0, name)

    held = {}

    def alongside(hop, got):
        if hop == 0:
            query_slots(1)
            query_slots(2)
            (got,) = with_queries(got)
        if hop == 1:
            early = project_queries(None, range(cut), keep, F32, "q_early")
            for step in range(3, up_last + 1):
                query_slots(step)
            got, held["q"] = tie(got, early)
        if hop == 2:
            late = project_queries(held["q"], range(cut, count), keep_features, BF, "q_late")
            got, held["q"] = tie(got, late)
        return got

    states, sums = payload[:, :HEAD], payload[:, HEAD : HEAD + 8]
    total = jnp.concatenate([*running_total(states, sums, count, alongside), sums], axis=1)
    out = attend(meta, held["q"], total, core_swap(total), heads_here, block)
    return out.reshape(frame_count, band_rows, column_count, HEADS * HEAD)


def gathered_form(latents, proj_weight):
    frame_count, band_rows, column_count, channels = latents.shape
    shard_rows = proj_weight.shape[0]
    band_count, band = lax.axis_size("space"), lax.axis_index("space")
    heads_here = HEADS // band_count
    own = proj_weight.reshape(shard_rows, 3, band_count, heads_here * HEAD)
    own = lax.dynamic_index_in_dim(own, band, 2, keepdims=False)
    own = own.reshape(shard_rows, 3 * heads_here * HEAD)
    weight = lax.all_gather(own, "tm", axis=0, tiled=True)
    tokens = lax.all_gather(latents, "space", axis=1, tiled=True)
    joined = tokens.shape[1]
    projected = dot(tokens.reshape(-1, channels), weight).astype(BF)
    split = projected.reshape(-1, 3, heads_here, HEAD)
    queries, feats, values = jax.nn.relu(split[:, 0]), jax.nn.relu(split[:, 1]), split[:, 2]
    states = jnp.einsum("nhe,nhf->hef", feats, values, preferred_element_type=F32)
    key_sums = jnp.sum(feats, axis=0, dtype=F32)
    states, key_sums = running_total(states, key_sums[:, :, None], lax.axis_size("tm"))
    states, key_sums = states.astype(BF), key_sums[:, :, 0]
    numerator = jnp.einsum("nhe,hef->nhf", queries, states, preferred_element_type=F32)
    denominator = jnp.einsum(
        "nhe,he->nh", queries.astype(F32), key_sums, precision=lax.Precision.HIGHEST
    )
    out = (numerator / (denominator[:, :, None] + 1.0)).astype(BF)
    out = out.reshape(frame_count, joined, column_count, heads_here * HEAD)
    return lax.all_to_all(out, "space", split_axis=1, concat_axis=3, tiled=True)


def on_device(latents, proj_weight):
    even = lax.axis_size("groups") % 2 == 0 and lax.axis_size("space") == 2
    if even and proj_weight.shape[0] // DEPTH == 1 and lax.axis_size("tm") > 2:
        return ring_form(latents, proj_weight)
    return gathered_form(latents, proj_weight)


def solution(mesh):
    return jax.shard_map(
        on_device,
        mesh=mesh,
        in_specs=(P(("groups", "tm"), "space", None, None), P("tm", None)),
        out_specs=P(("groups", "tm"), "space", None, None),
        check_vma=False,
    )
```

```python
import functools

import jax
import jax.numpy as jnp
import numpy as np
from jax import lax
from jax.experimental import pallas as pl
from jax.experimental.pallas import tpu as pltpu
from jax.sharding import PartitionSpec as P

HEADS = 10
HEAD = 112
LANES = 128
DEPTH = 256
BF = jnp.bfloat16
F32 = jnp.float32
LIMIT = 16 * 1024 * 1024


def ceil_to(value, step):
    return -(-value // step) * step


def dot(a, b):
    return jnp.dot(a, b, preferred_element_type=F32)


def params():
    return pltpu.CompilerParams(vmem_limit_bytes=LIMIT, dimension_semantics=("arbitrary",))


def cost(flops, moved):
    return pl.CostEstimate(flops=int(flops), bytes_accessed=int(moved), transcendentals=0)


def whole(shape):
    return pl.BlockSpec(shape, lambda i, *_: (0,) * len(shape))


def ring_order(count):
    if count % 2:
        return list(range(count))
    return list(range(0, count, 2)) + list(range(count - 1, 0, -2))


def slot_table(count):
    order = ring_order(count)
    up, down = count // 2, (count - 1) // 2
    table = np.zeros((count, count), np.int32)
    for at, index in enumerate(order):
        slots = [0]
        for step in range(1, up + 1):
            slots.append(-step)
            if step <= down:
                slots.append(step)
        table[index] = [order[(at + s) % count] for s in slots]
    return table


def split_rows(rows):
    third = DEPTH // 48 * 16
    spare = ceil_to((rows - DEPTH + 1) // 2, 16)
    return third, DEPTH - 2 * third, spare


def resident(kernel, meta, operands, outs, scratch, flops, name, aliases=None):
    in_vmem = pl.BlockSpec(memory_space=pltpu.VMEM)
    return pl.pallas_call(
        kernel,
        in_specs=[pl.BlockSpec(memory_space=pltpu.SMEM)] + [in_vmem] * len(operands),
        out_specs=[in_vmem] * len(outs),
        out_shape=outs,
        scratch_shapes=scratch,
        input_output_aliases=aliases or {},
        compiler_params=pltpu.CompilerParams(vmem_limit_bytes=LIMIT),
        cost_estimate=cost(flops, 0),
        name=name,
    )(meta, *operands)


def key_value_columns(meta, heads_here, run):
    wide, model = heads_here * HEAD, HEADS * HEAD

    def on_core(core):
        for part in (1, 2):
            begin = part * model + core * wide
            run(slice(begin, begin + wide), slice((part - 1) * wide, part * wide))

    for core in range(HEADS // heads_here):
        pl.when(meta[1] == core)(functools.partial(on_core, core))


def pack_first_kernel(meta, w_ref, up_ref, down_ref, *, heads_here):
    rows = w_ref.shape[0]
    third, shared, spare = split_rows(rows)
    own, other = (pl.ds(pl.multiple_of(p * third, 16), third) for p in (meta[0], 1 - meta[0]))
    end = up_ref.shape[0]
    blank = 2 * spare - (rows - DEPTH)
    common = shared + 2 * spare
    for ref, at in ((up_ref, end - blank), (down_ref, common - blank)):
        ref[at : at + blank, :] = jnp.zeros((blank, ref.shape[1]), BF)

    def run(of, to):
        for ref, take, at, common_at in ((up_ref, own, 0, third), (down_ref, other, common, 0)):
            ref[at : at + third, to] = w_ref[take, of]
            ref[common_at : common_at + common - blank, to] = w_ref[2 * third :, of]

    key_value_columns(meta, heads_here, run)


def pack_rest_kernel(meta, w_ref, after_ref, mine_ref, theirs_ref):
    rows = w_ref.shape[0]
    spare = split_rows(rows)[2]
    half, model = DEPTH // 2, HEADS * HEAD

    def queries(out_ref, core):
        out_ref[:half, :] = w_ref[core * half : (core + 1) * half, :model]
        out_ref[half:, :] = jnp.zeros((spare, model), BF)
        begin = DEPTH + core * spare
        count = min(spare, rows - begin)
        out_ref[half : half + count, :] = w_ref[begin : begin + count, :model]

    for core in range(2):
        pl.when(meta[1] == core)(functools.partial(queries, mine_ref, core))
        pl.when(meta[1] == 1 - core)(functools.partial(queries, theirs_ref, core))


def pack_first(meta, w, heads_here):
    third, shared, spare = split_rows(w.shape[0])
    out = jax.ShapeDtypeStruct((third + shared + 2 * spare, 2 * heads_here * HEAD), BF)
    kernel = functools.partial(pack_first_kernel, heads_here=heads_here)
    return resident(kernel, meta, [w], [out] * 2, [], 1e9, "pack_first")


def pack_rest(meta, w, after):
    half = DEPTH // 2 + split_rows(w.shape[0])[2]
    outs = [jax.ShapeDtypeStruct((half, HEADS * HEAD), BF)] * 2
    return resident(pack_rest_kernel, meta, [w, after], outs, [], 1e9, "pack_rest")


def pack_tokens_kernel(x_ref, after_ref, o_ref, *, rows, count):
    spare = split_rows(rows)[2]
    rest = rows - DEPTH
    blank = jnp.zeros((x_ref.shape[0], 2 * spare - rest), x_ref.dtype)
    left_over = []
    for j in range(count):
        at = j * rows
        o_ref[:, j * DEPTH : (j + 1) * DEPTH] = x_ref[:, at : at + DEPTH]
        left_over += [x_ref[:, at + DEPTH : at + rows], blank]
    o_ref[:, count * DEPTH :] = jnp.concatenate(left_over, axis=1)


def pack_tokens(x, after, rows, count, block):
    tokens, channels = x.shape
    depth = count * (DEPTH + 2 * split_rows(rows)[2])
    return pl.pallas_call(
        functools.partial(pack_tokens_kernel, rows=rows, count=count),
        grid=(tokens // block,),
        in_specs=[
            pl.BlockSpec((block, channels), lambda i: (i, 0)),
            pl.BlockSpec(memory_space=pl.ANY),
        ],
        out_specs=pl.BlockSpec((block, depth), lambda i: (i, 0)),
        out_shape=jax.ShapeDtypeStruct((tokens, depth), BF),
        compiler_params=params(),
        cost_estimate=cost(0, 4 * x.size),
        name="pack_tokens",
    )(x, after)


def put(weights, at, step, value):
    weights[pl.ds(pl.multiple_of(at, step), value.shape[0]), :] = value


def put_rows(weights, at, piece, begin, end):
    offset = 0
    for ref, first, count in piece:
        low, high = max(begin, offset), min(end, offset + count)
        if low < high:
            put(weights, at + low - begin, 16, ref[first + low - offset : first + high - offset, :])
        offset += count


def fill_keys_values(weights, meta, slots, pieces, rows):
    third, shared, _ = split_rows(rows)
    for s in range(len(slots)):
        own, other, common = pieces[3 * s : 3 * s + 3]
        put_rows(weights, s * DEPTH + meta[0] * third, own, 0, third)
        put_rows(weights, s * DEPTH + (1 - meta[0]) * third, other, 0, third)
        put_rows(weights, s * DEPTH + 2 * third, common, 0, shared)


def fill_queries(weights, meta, slots, pieces, rows):
    half = DEPTH // 2
    for s in range(len(slots)):
        for piece, core in zip(pieces[2 * s : 2 * s + 2], (meta[1], 1 - meta[1])):
            put_rows(weights, s * DEPTH + core * half, piece, 0, half)


def fill_left_over(weights, meta, base, pieces, rows, of_keys):
    third, shared, spare = split_rows(rows)
    if of_keys:
        for s, piece in enumerate(pieces):
            at = base + meta[2 + s] * 2 * spare
            put_rows(weights, at, piece, shared, shared + 2 * spare)
        return
    half = DEPTH // 2
    for s in range(len(pieces) // 2):
        for piece, core in zip(pieces[2 * s : 2 * s + 2], (meta[1], 1 - meta[1])):
            put_rows(weights, base + (meta[2 + s] * 2 + core) * spare, piece, half, half + spare)


def token_columns(x_ref, rows, meta, slots, count, with_rest):
    taken = [x_ref[rows, pl.ds(pl.multiple_of(meta[2 + s] * DEPTH, DEPTH), DEPTH)] for s in slots]
    if with_rest:
        taken.append(x_ref[rows, count * DEPTH :])
    return jnp.concatenate(taken, axis=1)


def every_block(xs, block, run):
    tokens = xs[0].shape[0]
    for band, x_ref in enumerate(xs):

        def step(i, carry, band=band, x_ref=x_ref):
            at = pl.multiple_of(i * block, block)
            run(x_ref, pl.ds(at, block), pl.ds(pl.multiple_of(at + band * tokens, block), block))
            return carry

        lax.fori_loop(0, tokens // block, step, 0)


def project_kernel(meta, *refs, plan, where, finish):
    bands_in, slots, count, rows, of_keys, has_acc, with_rest, block = plan
    xs, refs = refs[:bands_in], refs[bands_in:]
    acc_ref, refs = (refs[0], refs[1:]) if has_acc else (None, refs)
    pieces, rest_pieces = (
        [[(refs[i], at, n) for i, at, n in piece] for piece in pieces] for pieces in where
    )
    refs = refs[1 + max(i for pieces in where for piece in pieces for i, _, _ in piece) :]
    weights, refs = refs[-1], refs[:-1]
    (fill_keys_values if of_keys else fill_queries)(weights, meta, slots, pieces, rows)
    if with_rest:
        fill_left_over(weights, meta, len(slots) * DEPTH, rest_pieces, rows, of_keys)

    def run(x_ref, rows_here, rows_of_all):
        x = token_columns(x_ref, rows_here, meta, slots, count, with_rest)
        total = dot(x, weights[...])
        if has_acc:
            total = total + acc_ref[rows_of_all, :]
        finish(refs, total, rows_of_all)

    every_block(xs, block, run)


def keep(refs, total, rows):
    refs[0][rows, :] = total


def keep_features(refs, total, rows):
    refs[0][rows, :] = jnp.maximum(total.astype(BF), 0)


def distinct(*lists):
    arrays, places = [], {}
    for array, _, _ in (part for pieces in lists for piece in pieces for part in piece):
        if id(array) not in places:
            places[id(array)] = len(arrays)
            arrays.append(array)
    where = tuple(
        tuple(tuple((places[id(a)], at, n) for a, at, n in piece) for piece in pieces)
        for pieces in lists
    )
    return arrays, where


def project(meta, xs, acc, pieces, rest_pieces, plan, finish, out, name):
    bands_in, slots, count, rows, of_keys, has_acc, with_rest, block = plan
    arrays, where = distinct(pieces, rest_pieces)
    wide = arrays[0].shape[1]
    depth = len(slots) * DEPTH + with_rest * count * 2 * split_rows(rows)[2]
    tokens = bands_in * xs[0].shape[0]
    operands = [*xs, *([acc] if has_acc else []), *arrays]
    in_place = has_acc and out.shape == acc.shape and out.dtype == acc.dtype
    return resident(
        functools.partial(project_kernel, plan=plan, where=where, finish=finish),
        meta,
        operands,
        [out],
        [pltpu.VMEM((depth, wide), BF)],
        2 * tokens * depth * wide,
        name,
        {1 + bands_in: 0} if in_place else None,
    )[0]


def states_kernel(meta, *refs, plan, where, heads_here):
    out_ref, values, weights = refs[-3:]
    wide = heads_here * HEAD
    values[...] = jnp.ones_like(values)
    out_ref[...] = jnp.zeros_like(out_ref)

    def finish(_, projected, rows):
        projected = projected.astype(BF)
        feats = jnp.maximum(projected[:, :wide], 0).T
        for h in range(heads_here):
            rows = slice(h * HEAD, (h + 1) * HEAD)
            values[:, :HEAD] = projected[:, wide + h * HEAD : wide + (h + 1) * HEAD]
            out_ref[rows, :] += dot(feats[rows, :], values[...])

    project_kernel(meta, *refs, plan=plan, where=where, finish=finish)


def block_states(meta, xs, acc, pieces, rest_pieces, plan, heads_here):
    wide = heads_here * HEAD
    bands_in, slots, count, rows, _, has_acc, with_rest, block = plan
    depth = len(slots) * DEPTH + with_rest * count * 2 * split_rows(rows)[2]
    tokens = bands_in * xs[0].shape[0]
    arrays, where = distinct(pieces, rest_pieces)
    return resident(
        functools.partial(states_kernel, plan=plan, where=where, heads_here=heads_here),
        meta,
        [*xs, acc, *arrays],
        [jax.ShapeDtypeStruct((wide, LANES), F32)],
        [
            pltpu.VMEM((block, LANES), BF),
            pltpu.VMEM((depth, 2 * wide), BF),
        ],
        2 * tokens * (depth * 2 * wide + wide * LANES),
        "states",
    )[0]


def bands():
    model = HEADS * HEAD
    found = []
    for left in range(0, model, 256):
        right = min(left + 256, model)
        heads = range(left // HEAD, -(-right // HEAD))
        low = heads[0] * HEAD // LANES * LANES
        high = min(ceil_to((heads[-1] + 1) * HEAD, LANES), model)
        found.append((left, right, low, high, heads))
    return found


def attend_kernel(
    meta, q_ref, mine_ref, theirs_ref, out_hbm, states, sums, held, sems, *, heads_here
):
    states[...] = jnp.zeros_like(states)
    mine, theirs = mine_ref[...], theirs_ref[...]
    parts = [jnp.where(meta[1] == k, mine, theirs) for k in range(HEADS // heads_here)]
    base = 0
    for left, right, low, high, heads in bands():
        for h in heads:
            at = (h % heads_here) * HEAD
            begin, end = max(h * HEAD, left), min((h + 1) * HEAD, right)
            rows = slice(base + h * HEAD - low, base + (h + 1) * HEAD - low)
            block = parts[h // heads_here][at : at + HEAD, begin - h * HEAD : end - h * HEAD]
            states[rows, begin - left : end - left] = block.astype(BF)
        base += high - low
    lane = lax.broadcasted_iota(jnp.int32, (HEAD, LANES), 1)
    for h in range(HEADS):
        at = (h % heads_here) * HEAD
        key_sums = parts[h // heads_here][at : at + HEAD, HEAD : HEAD + 1]
        key_sums = jnp.broadcast_to(key_sums, (HEAD, LANES))
        upper = key_sums.astype(BF).astype(F32)
        chosen = jnp.where(lane == h, upper, jnp.where(lane == h + 64, key_sums - upper, 0.0))
        sums[h * HEAD : (h + 1) * HEAD, :] = chosen.astype(BF)
    blocks, block = held.shape[0], held.shape[1]
    column = lax.broadcasted_iota(jnp.int32, (block, LANES), 1)
    shares = []
    for i in range(blocks):
        total = dot(q_ref[i * block : (i + 1) * block, :], sums[...])
        shares.append(1.0 / (total + pltpu.roll(total, 64, 1) + 1.0))

    def send(i):
        return pltpu.make_async_copy(held.at[i], out_hbm.at[pl.ds(i * block, block)], sems.at[i])

    for i in range(blocks):
        base = 0
        for left, right, low, high, _ in bands():
            q = q_ref[i * block : (i + 1) * block, low:high]
            numerator = dot(q, states[base : base + high - low, :])
            for at in range(left, right, LANES):
                width = min(LANES, right - at)
                head = sum((column + at >= h * HEAD).astype(jnp.int32) for h in range(1, HEADS))
                scale = jnp.take_along_axis(shares[i], head, axis=1)
                scaled = (numerator[:, at - left : at - left + LANES] * scale).astype(BF)
                held[i, :, at : at + width] = scaled[:, :width]
            base += high - low
        send(i).start()
    for i in range(blocks):
        send(i).wait()


def attend(meta, queries, mine, theirs, heads_here, block):
    tokens, model = queries.shape
    rows = sum(high - low for _, _, low, high, _ in bands())
    in_vmem = pl.BlockSpec(memory_space=pltpu.VMEM)
    return pl.pallas_call(
        functools.partial(attend_kernel, heads_here=heads_here),
        in_specs=[pl.BlockSpec(memory_space=pltpu.SMEM)] + [in_vmem] * 3,
        out_specs=pl.BlockSpec(memory_space=pl.ANY),
        scratch_shapes=[
            pltpu.VMEM((rows, 256), BF),
            pltpu.VMEM((model, LANES), BF),
            pltpu.VMEM((tokens // block, block, model), BF),
            pltpu.SemaphoreType.DMA((tokens // block,)),
        ],
        out_shape=jax.ShapeDtypeStruct((tokens, model), BF),
        compiler_params=pltpu.CompilerParams(vmem_limit_bytes=LIMIT),
        cost_estimate=cost(2 * tokens * model * 800, tokens * model * 4),
        name="attend",
    )(meta, queries, mine, theirs)


def swap_pairs(count):
    return [(i, i ^ 1) for i in range(count)]


def ring_steps(count):
    order = ring_order(count)
    forward = [(order[i], order[(i + 1) % count]) for i in range(count)]
    return forward, [(b, a) for a, b in forward]


def running_total(states, sums, count, alongside=None):
    reach, hop = 1, 0
    wide, room = states.shape[-1], sums.shape[-1]
    while reach < count:
        pairs = [(i, i + reach) for i in range(count - reach)]
        upper = sums.astype(BF)
        lower = (sums - upper.astype(F32)).astype(BF)
        sent = jnp.concatenate([states.astype(BF), upper, lower], axis=-1)
        got = lax.ppermute(sent, "tm", pairs)
        if alongside is not None:
            got = alongside(hop, got)
        got = got.astype(F32)
        states = states + got[..., :wide]
        sums = sums + (got[..., wide : wide + room] + got[..., wide + room :])
        reach, hop = reach * 2, hop + 1
    return states, sums


def tie(*values):
    return lax.optimization_barrier(values)


def ring_form(latents, proj_weight):
    frame_count, band_rows, column_count, channels = latents.shape
    rows = proj_weight.shape[0]
    third, shared, spare = split_rows(rows)
    common_rows = shared + 2 * spare
    count, groups = lax.axis_size("tm"), lax.axis_size("groups")
    heads_here = HEADS // 2
    tokens = frame_count * band_rows * column_count
    block = 960 if tokens % 960 == 0 else tokens
    small = 240 if tokens % 240 == 0 else tokens

    forward, backward = ring_steps(count)
    across, over = swap_pairs(groups), swap_pairs(2)
    last = count // 2

    def ring(value, up):
        return lax.ppermute(value, "tm", forward if up else backward)

    def plane_swap(up, down):
        value = jnp.concatenate([up[:third], down[common_rows:]], axis=0)
        return lax.ppermute(value, "groups", across)

    def core_swap(value):
        return lax.ppermute(value, "space", over)

    here = jnp.asarray(slot_table(count))[lax.axis_index("tm")]
    plane = lax.rem(lax.axis_index("groups"), 2)
    meta = jnp.concatenate([jnp.stack([plane, lax.axis_index("space")]), here]).astype(jnp.int32)

    up, down = pack_first(meta, proj_weight, heads_here)
    mine, theirs = pack_rest(meta, proj_weight, up)
    x = pack_tokens(latents.reshape(tokens, channels), mine, rows, count, small)

    ways = [(mine, mine)]
    half = DEPTH // 2 + spare
    mid = half // 2 // 16 * 16 + 16

    def next_queries():
        if len(ways) < last:
            ways.append((ring(ways[-1][0], True), ring(ways[-1][1], False)))
        elif len(ways) == last:
            ways.append((ring(ways[-1][0][:mid], True), ring(ways[-1][1][mid:], False)))

    def with_queries(*values):
        *values, up, down = tie(*values, *ways[-1])
        ways[-1] = up, down
        next_queries()
        return values

    def plan(bands_in, which, of_keys, has_acc, with_rest):
        return (bands_in, tuple(which), count, rows, of_keys, has_acc, with_rest, block)

    kv_shape = jax.ShapeDtypeStruct((2 * tokens, 2 * heads_here * HEAD), F32)

    def add_keys_values(acc, which):
        pieces = [part for s in which for part in slots[s]]
        settings = plan(2, which, True, acc is not None, False)
        return project(meta, both, acc, pieces, [], settings, keep, kv_shape, "kv_part")

    def thirds(up, down, up_other, down_other):
        common_up, common_down = [(up, third, common_rows)], [(down, 0, common_rows)]
        return [
            [[(up, 0, third)], [up_other], common_up],
            [[down_other], [(down, common_rows, third)], common_down],
        ]

    slots = thirds(up, down, (down, common_rows, third), (up, 0, third))[:1]
    some = common_rows // 2 // 16 * 16
    swapped, acc = None, None
    for step in range(1, last + 1):
        before = up, down
        full = step < last
        up = ring(up if full else up[: third + some], True)
        down = ring(down if full else down[some:], False)
        if step == 1:
            x = tie(x, up, down)[0]
            x_other = core_swap(x)
            both = (x, x_other)
        elif full:
            x_other, up, down, swapped = tie(x_other, up, down, swapped)
            both = (x, x_other)
        else:
            acc = add_keys_values(None, range(len(slots)))
            acc, up, down, swapped = with_queries(acc, up, down, swapped)
        if step > 1:
            slots += thirds(*before, (swapped, 0, third), (swapped, third, third))
        if full:
            swapped = plane_swap(up, down)
        if step + 1 == last:
            next_queries()
    rest = common_rows - some
    slots.append([[(up, 0, third)], [(down, rest, third)], [(up, third, some), (down, 0, rest)]])
    settings = plan(2, range(count - 3, count), True, True, True)
    pieces = [piece for slot in slots[count - 3 :] for piece in slot]
    commons = [slot[2] for slot in slots]
    payload = block_states(meta, both, acc, pieces, commons, settings, heads_here)
    (payload,) = with_queries(payload)

    found = [[[(mine, 0, half)], [(theirs, 0, half)]]]
    cut = 1 + 2 * ((count - 1) // 4 + (count > 4))

    def query_slots(step):
        if step < last:
            for value in ways[step]:
                found.append([[(value, 0, half)], [(core_swap(value), 0, half)]])
        else:
            value = jnp.concatenate(ways[step], axis=0)
            found.append([[(value, 0, half)], [(core_swap(value), 0, half)]])

    def project_queries(acc, which, finish, dtype, name):
        ends = which[-1] == count - 1
        pieces = [part for s in which for part in found[s]]
        every = [part for s in found for part in s] if ends else []
        settings = plan(1, which, False, acc is not None, ends)
        out = jax.ShapeDtypeStruct((tokens, HEADS * HEAD), dtype)
        return project(meta, (x,), acc, pieces, every, settings, finish, out, name)

    held = {}

    def alongside(hop, got):
        if hop == 0:
            query_slots(1)
            query_slots(2)
            (got,) = with_queries(got)
        if hop == 1:
            early = project_queries(None, range(cut), keep, F32, "q_early")
            query_slots(3)
            got, held["q"] = tie(got, early)
        if hop == 2:
            query_slots(4)
            late = project_queries(held["q"], range(cut, count), keep_features, BF, "q_late")
            got, held["q"] = tie(got, late)
        return got

    states, sums = payload[:, :HEAD], payload[:, HEAD : HEAD + 8]
    total = jnp.concatenate([*running_total(states, sums, count, alongside), sums], axis=1)
    out = attend(meta, held["q"], total, core_swap(total), heads_here, small)
    return out.reshape(frame_count, band_rows, column_count, HEADS * HEAD)


def gathered_form(latents, proj_weight):
    frame_count, band_rows, column_count, channels = latents.shape
    shard_rows = proj_weight.shape[0]
    band_count, band = lax.axis_size("space"), lax.axis_index("space")
    heads_here = HEADS // band_count
    own = proj_weight.reshape(shard_rows, 3, band_count, heads_here * HEAD)
    own = lax.dynamic_index_in_dim(own, band, 2, keepdims=False)
    own = own.reshape(shard_rows, 3 * heads_here * HEAD)
    weight = lax.all_gather(own, "tm", axis=0, tiled=True)
    tokens = lax.all_gather(latents, "space", axis=1, tiled=True)
    joined = tokens.shape[1]
    projected = dot(tokens.reshape(-1, channels), weight).astype(BF)
    split = projected.reshape(-1, 3, heads_here, HEAD)
    queries, feats, values = jax.nn.relu(split[:, 0]), jax.nn.relu(split[:, 1]), split[:, 2]
    states = jnp.einsum("nhe,nhf->hef", feats, values, preferred_element_type=F32)
    key_sums = jnp.sum(feats, axis=0, dtype=F32)
    states, key_sums = running_total(states, key_sums[:, :, None], lax.axis_size("tm"))
    states, key_sums = states.astype(BF), key_sums[:, :, 0]
    numerator = jnp.einsum("nhe,hef->nhf", queries, states, preferred_element_type=F32)
    denominator = jnp.einsum(
        "nhe,he->nh", queries.astype(F32), key_sums, precision=lax.Precision.HIGHEST
    )
    out = (numerator / (denominator[:, :, None] + 1.0)).astype(BF)
    out = out.reshape(frame_count, joined, column_count, heads_here * HEAD)
    return lax.all_to_all(out, "space", split_axis=1, concat_axis=3, tiled=True)


def on_device(latents, proj_weight):
    even = lax.axis_size("groups") % 2 == 0 and lax.axis_size("space") == 2
    if even and proj_weight.shape[0] // DEPTH == 1 and lax.axis_size("tm") == 8:
        return ring_form(latents, proj_weight)
    return gathered_form(latents, proj_weight)


def solution(mesh):
    return jax.shard_map(
        on_device,
        mesh=mesh,
        in_specs=(P(("groups", "tm"), "space", None, None), P("tm", None)),
        out_specs=P(("groups", "tm"), "space", None, None),
        check_vma=False,
    )
```

```python
import functools

import jax
import jax.numpy as jnp
import numpy as np
from jax import lax
from jax.experimental import pallas as pl
from jax.experimental.pallas import tpu as pltpu
from jax.sharding import PartitionSpec as P

HEADS = 10
HEAD = 112
LANES = 128
DEPTH = 256
BF = jnp.bfloat16
F32 = jnp.float32
LIMIT = 16 * 1024 * 1024


def ceil_to(value, step):
    return -(-value // step) * step


def dot(a, b):
    return jnp.dot(a, b, preferred_element_type=F32)


def params():
    return pltpu.CompilerParams(vmem_limit_bytes=LIMIT, dimension_semantics=("arbitrary",))


def cost(flops, moved):
    return pl.CostEstimate(flops=int(flops), bytes_accessed=int(moved), transcendentals=0)


def whole(shape):
    return pl.BlockSpec(shape, lambda i, *_: (0,) * len(shape))


def ring_order(count):
    if count % 2:
        return list(range(count))
    return list(range(0, count, 2)) + list(range(count - 1, 0, -2))


def slot_table(count):
    order = ring_order(count)
    up, down = count // 2, (count - 1) // 2
    table = np.zeros((count, count), np.int32)
    for at, index in enumerate(order):
        slots = [0]
        for step in range(1, up + 1):
            slots.append(-step)
            if step <= down:
                slots.append(step)
        table[index] = [order[(at + s) % count] for s in slots]
    return table


def split_rows(rows):
    third = DEPTH // 48 * 16
    spare = ceil_to((rows - DEPTH + 1) // 2, 16)
    return third, DEPTH - 2 * third, spare


def resident(kernel, meta, operands, outs, scratch, flops, name, aliases=None):
    in_vmem = pl.BlockSpec(memory_space=pltpu.VMEM)
    return pl.pallas_call(
        kernel,
        in_specs=[pl.BlockSpec(memory_space=pltpu.SMEM)] + [in_vmem] * len(operands),
        out_specs=[in_vmem] * len(outs),
        out_shape=outs,
        scratch_shapes=scratch,
        input_output_aliases=aliases or {},
        compiler_params=pltpu.CompilerParams(vmem_limit_bytes=LIMIT),
        cost_estimate=cost(flops, 0),
        name=name,
    )(meta, *operands)


def key_value_columns(meta, heads_here, run):
    wide, model = heads_here * HEAD, HEADS * HEAD

    def on_core(core):
        for part in (1, 2):
            begin = part * model + core * wide
            run(slice(begin, begin + wide), slice((part - 1) * wide, part * wide))

    for core in range(HEADS // heads_here):
        pl.when(meta[1] == core)(functools.partial(on_core, core))


def pack_first_kernel(meta, w_ref, up_ref, down_ref, *, heads_here):
    rows = w_ref.shape[0]
    third, shared, spare = split_rows(rows)
    own, other = (pl.ds(pl.multiple_of(p * third, 16), third) for p in (meta[0], 1 - meta[0]))
    end = up_ref.shape[0]
    blank = 2 * spare - (rows - DEPTH)
    common = shared + 2 * spare
    for ref, at in ((up_ref, end - blank), (down_ref, common - blank)):
        ref[at : at + blank, :] = jnp.zeros((blank, ref.shape[1]), BF)

    def run(of, to):
        for ref, take, at, common_at in ((up_ref, own, 0, third), (down_ref, other, common, 0)):
            ref[at : at + third, to] = w_ref[take, of]
            ref[common_at : common_at + common - blank, to] = w_ref[2 * third :, of]

    key_value_columns(meta, heads_here, run)


def pack_rest_kernel(meta, w_ref, after_ref, mine_ref, theirs_ref):
    rows = w_ref.shape[0]
    spare = split_rows(rows)[2]
    half, model = DEPTH // 2, HEADS * HEAD

    def queries(out_ref, core):
        out_ref[:half, :] = w_ref[core * half : (core + 1) * half, :model]
        out_ref[half:, :] = jnp.zeros((spare, model), BF)
        begin = DEPTH + core * spare
        count = min(spare, rows - begin)
        out_ref[half : half + count, :] = w_ref[begin : begin + count, :model]

    for core in range(2):
        pl.when(meta[1] == core)(functools.partial(queries, mine_ref, core))
        pl.when(meta[1] == 1 - core)(functools.partial(queries, theirs_ref, core))


def pack_first(meta, w, heads_here):
    third, shared, spare = split_rows(w.shape[0])
    out = jax.ShapeDtypeStruct((third + shared + 2 * spare, 2 * heads_here * HEAD), BF)
    kernel = functools.partial(pack_first_kernel, heads_here=heads_here)
    return resident(kernel, meta, [w], [out] * 2, [], 1e9, "pack_first")


def pack_rest(meta, w, after):
    half = DEPTH // 2 + split_rows(w.shape[0])[2]
    outs = [jax.ShapeDtypeStruct((half, HEADS * HEAD), BF)] * 2
    return resident(pack_rest_kernel, meta, [w, after], outs, [], 1e9, "pack_rest")


def pack_tokens_kernel(x_ref, after_ref, o_ref, *, rows, count):
    spare = split_rows(rows)[2]
    rest = rows - DEPTH
    blank = jnp.zeros((x_ref.shape[0], 2 * spare - rest), x_ref.dtype)
    left_over = []
    for j in range(count):
        at = j * rows
        o_ref[:, j * DEPTH : (j + 1) * DEPTH] = x_ref[:, at : at + DEPTH]
        left_over += [x_ref[:, at + DEPTH : at + rows], blank]
    o_ref[:, count * DEPTH :] = jnp.concatenate(left_over, axis=1)


def pack_tokens(x, after, rows, count, block):
    tokens, channels = x.shape
    depth = count * (DEPTH + 2 * split_rows(rows)[2])
    return pl.pallas_call(
        functools.partial(pack_tokens_kernel, rows=rows, count=count),
        grid=(tokens // block,),
        in_specs=[
            pl.BlockSpec((block, channels), lambda i: (i, 0)),
            pl.BlockSpec(memory_space=pl.ANY),
        ],
        out_specs=pl.BlockSpec((block, depth), lambda i: (i, 0)),
        out_shape=jax.ShapeDtypeStruct((tokens, depth), BF),
        compiler_params=params(),
        cost_estimate=cost(0, 4 * x.size),
        name="pack_tokens",
    )(x, after)


def put(weights, at, step, value):
    weights[pl.ds(pl.multiple_of(at, step), value.shape[0]), :] = value


def put_rows(weights, at, piece, begin, end):
    offset = 0
    for ref, first, count in piece:
        low, high = max(begin, offset), min(end, offset + count)
        if low < high:
            put(weights, at + low - begin, 16, ref[first + low - offset : first + high - offset, :])
        offset += count


def fill_keys_values(weights, meta, slots, pieces, rows):
    third, shared, _ = split_rows(rows)
    for s in range(len(slots)):
        own, other, common = pieces[3 * s : 3 * s + 3]
        put_rows(weights, s * DEPTH + meta[0] * third, own, 0, third)
        put_rows(weights, s * DEPTH + (1 - meta[0]) * third, other, 0, third)
        put_rows(weights, s * DEPTH + 2 * third, common, 0, shared)


def fill_queries(weights, meta, slots, pieces, rows):
    half = DEPTH // 2
    for s in range(len(slots)):
        for piece, core in zip(pieces[2 * s : 2 * s + 2], (meta[1], 1 - meta[1])):
            put_rows(weights, s * DEPTH + core * half, piece, 0, half)


def fill_left_over(weights, meta, base, pieces, rows, of_keys):
    third, shared, spare = split_rows(rows)
    if of_keys:
        for s, piece in enumerate(pieces):
            at = base + meta[2 + s] * 2 * spare
            put_rows(weights, at, piece, shared, shared + 2 * spare)
        return
    half = DEPTH // 2
    for s in range(len(pieces) // 2):
        for piece, core in zip(pieces[2 * s : 2 * s + 2], (meta[1], 1 - meta[1])):
            put_rows(weights, base + (meta[2 + s] * 2 + core) * spare, piece, half, half + spare)


def token_columns(x_ref, rows, meta, slots, count, with_rest):
    taken = [x_ref[rows, pl.ds(pl.multiple_of(meta[2 + s] * DEPTH, DEPTH), DEPTH)] for s in slots]
    if with_rest:
        taken.append(x_ref[rows, count * DEPTH :])
    return jnp.concatenate(taken, axis=1)


def every_block(xs, block, run):
    tokens = xs[0].shape[0]
    for band, x_ref in enumerate(xs):

        def step(i, carry, band=band, x_ref=x_ref):
            at = pl.multiple_of(i * block, block)
            run(x_ref, pl.ds(at, block), pl.ds(pl.multiple_of(at + band * tokens, block), block))
            return carry

        lax.fori_loop(0, tokens // block, step, 0)


def project_kernel(meta, *refs, plan, where, finish):
    bands_in, slots, count, rows, of_keys, has_acc, with_rest, block = plan
    xs, refs = refs[:bands_in], refs[bands_in:]
    acc_ref, refs = (refs[0], refs[1:]) if has_acc else (None, refs)
    pieces, rest_pieces = (
        [[(refs[i], at, n) for i, at, n in piece] for piece in pieces] for pieces in where
    )
    refs = refs[1 + max(i for pieces in where for piece in pieces for i, _, _ in piece) :]
    weights, refs = refs[-1], refs[:-1]
    (fill_keys_values if of_keys else fill_queries)(weights, meta, slots, pieces, rows)
    if with_rest:
        fill_left_over(weights, meta, len(slots) * DEPTH, rest_pieces, rows, of_keys)

    def run(x_ref, rows_here, rows_of_all):
        x = token_columns(x_ref, rows_here, meta, slots, count, with_rest)
        total = dot(x, weights[...])
        if has_acc:
            total = total + acc_ref[rows_of_all, :]
        finish(refs, total, rows_of_all)

    every_block(xs, block, run)


def keep(refs, total, rows):
    refs[0][rows, :] = total


def keep_features(refs, total, rows):
    refs[0][rows, :] = jnp.maximum(total.astype(BF), 0)


def distinct(*lists):
    arrays, places = [], {}
    for array, _, _ in (part for pieces in lists for piece in pieces for part in piece):
        if id(array) not in places:
            places[id(array)] = len(arrays)
            arrays.append(array)
    where = tuple(
        tuple(tuple((places[id(a)], at, n) for a, at, n in piece) for piece in pieces)
        for pieces in lists
    )
    return arrays, where


def project(meta, xs, acc, pieces, rest_pieces, plan, finish, out, name):
    bands_in, slots, count, rows, of_keys, has_acc, with_rest, block = plan
    arrays, where = distinct(pieces, rest_pieces)
    wide = arrays[0].shape[1]
    depth = len(slots) * DEPTH + with_rest * count * 2 * split_rows(rows)[2]
    tokens = bands_in * xs[0].shape[0]
    operands = [*xs, *([acc] if has_acc else []), *arrays]
    in_place = has_acc and out.shape == acc.shape and out.dtype == acc.dtype
    return resident(
        functools.partial(project_kernel, plan=plan, where=where, finish=finish),
        meta,
        operands,
        [out],
        [pltpu.VMEM((depth, wide), BF)],
        2 * tokens * depth * wide,
        name,
        {1 + bands_in: 0} if in_place else None,
    )[0]


def states_kernel(meta, *refs, plan, where, heads_here):
    out_ref, values, weights = refs[-3:]
    wide = heads_here * HEAD
    values[...] = jnp.ones_like(values)
    out_ref[...] = jnp.zeros_like(out_ref)

    def finish(_, projected, rows):
        projected = projected.astype(BF)
        feats = jnp.maximum(projected[:, :wide], 0).T
        for h in range(heads_here):
            rows = slice(h * HEAD, (h + 1) * HEAD)
            values[:, :HEAD] = projected[:, wide + h * HEAD : wide + (h + 1) * HEAD]
            out_ref[rows, :] += dot(feats[rows, :], values[...])

    project_kernel(meta, *refs, plan=plan, where=where, finish=finish)


def block_states(meta, xs, acc, pieces, rest_pieces, plan, heads_here):
    wide = heads_here * HEAD
    bands_in, slots, count, rows, _, has_acc, with_rest, block = plan
    depth = len(slots) * DEPTH + with_rest * count * 2 * split_rows(rows)[2]
    tokens = bands_in * xs[0].shape[0]
    arrays, where = distinct(pieces, rest_pieces)
    return resident(
        functools.partial(states_kernel, plan=plan, where=where, heads_here=heads_here),
        meta,
        [*xs, acc, *arrays],
        [jax.ShapeDtypeStruct((wide, LANES), F32)],
        [
            pltpu.VMEM((block, LANES), BF),
            pltpu.VMEM((depth, 2 * wide), BF),
        ],
        2 * tokens * (depth * 2 * wide + wide * LANES),
        "states",
    )[0]


def bands():
    model = HEADS * HEAD
    found = []
    for left in range(0, model, 256):
        right = min(left + 256, model)
        heads = range(left // HEAD, -(-right // HEAD))
        low = heads[0] * HEAD // LANES * LANES
        high = min(ceil_to((heads[-1] + 1) * HEAD, LANES), model)
        found.append((left, right, low, high, heads))
    return found


def attend_kernel(
    meta, q_ref, mine_ref, theirs_ref, out_hbm, states, sums, held, sems, *, heads_here
):
    states[...] = jnp.zeros_like(states)
    mine, theirs = mine_ref[...], theirs_ref[...]
    parts = [jnp.where(meta[1] == k, mine, theirs) for k in range(HEADS // heads_here)]
    base = 0
    for left, right, low, high, heads in bands():
        for h in heads:
            at = (h % heads_here) * HEAD
            begin, end = max(h * HEAD, left), min((h + 1) * HEAD, right)
            rows = slice(base + h * HEAD - low, base + (h + 1) * HEAD - low)
            block = parts[h // heads_here][at : at + HEAD, begin - h * HEAD : end - h * HEAD]
            states[rows, begin - left : end - left] = block.astype(BF)
        base += high - low
    lane = lax.broadcasted_iota(jnp.int32, (HEAD, LANES), 1)
    for h in range(HEADS):
        at = (h % heads_here) * HEAD
        key_sums = parts[h // heads_here][at : at + HEAD, HEAD : HEAD + 1]
        key_sums = jnp.broadcast_to(key_sums, (HEAD, LANES))
        upper = key_sums.astype(BF).astype(F32)
        chosen = jnp.where(lane == h, upper, jnp.where(lane == h + 64, key_sums - upper, 0.0))
        sums[h * HEAD : (h + 1) * HEAD, :] = chosen.astype(BF)
    blocks, block = held.shape[0], held.shape[1]
    column = lax.broadcasted_iota(jnp.int32, (block, LANES), 1)
    shares = []
    for i in range(blocks):
        total = dot(q_ref[i * block : (i + 1) * block, :], sums[...])
        shares.append(1.0 / (total + pltpu.roll(total, 64, 1) + 1.0))

    def send(i):
        return pltpu.make_async_copy(held.at[i], out_hbm.at[pl.ds(i * block, block)], sems.at[i])

    for i in range(blocks):
        base = 0
        for left, right, low, high, _ in bands():
            q = q_ref[i * block : (i + 1) * block, low:high]
            numerator = dot(q, states[base : base + high - low, :])
            for at in range(left, right, LANES):
                width = min(LANES, right - at)
                head = sum((column + at >= h * HEAD).astype(jnp.int32) for h in range(1, HEADS))
                scale = jnp.take_along_axis(shares[i], head, axis=1)
                scaled = (numerator[:, at - left : at - left + LANES] * scale).astype(BF)
                held[i, :, at : at + width] = scaled[:, :width]
            base += high - low
        send(i).start()
    for i in range(blocks):
        send(i).wait()


def attend(meta, queries, mine, theirs, heads_here, block):
    tokens, model = queries.shape
    rows = sum(high - low for _, _, low, high, _ in bands())
    in_vmem = pl.BlockSpec(memory_space=pltpu.VMEM)
    return pl.pallas_call(
        functools.partial(attend_kernel, heads_here=heads_here),
        in_specs=[pl.BlockSpec(memory_space=pltpu.SMEM)] + [in_vmem] * 3,
        out_specs=pl.BlockSpec(memory_space=pl.ANY),
        scratch_shapes=[
            pltpu.VMEM((rows, 256), BF),
            pltpu.VMEM((model, LANES), BF),
            pltpu.VMEM((tokens // block, block, model), BF),
            pltpu.SemaphoreType.DMA((tokens // block,)),
        ],
        out_shape=jax.ShapeDtypeStruct((tokens, model), BF),
        compiler_params=pltpu.CompilerParams(vmem_limit_bytes=LIMIT),
        cost_estimate=cost(2 * tokens * model * 800, tokens * model * 4),
        name="attend",
    )(meta, queries, mine, theirs)


def swap_pairs(count):
    return [(i, i ^ 1) for i in range(count)]


def ring_steps(count):
    order = ring_order(count)
    forward = [(order[i], order[(i + 1) % count]) for i in range(count)]
    return forward, [(b, a) for a, b in forward]


def running_total(states, sums, count, alongside=None):
    reach, hop = 1, 0
    wide, room = states.shape[-1], sums.shape[-1]
    while reach < count:
        pairs = [(i, i + reach) for i in range(count - reach)]
        upper = sums.astype(BF)
        lower = (sums - upper.astype(F32)).astype(BF)
        sent = jnp.concatenate([states.astype(BF), upper, lower], axis=-1)
        got = lax.ppermute(sent, "tm", pairs)
        if alongside is not None:
            got = alongside(hop, got)
        got = got.astype(F32)
        states = states + got[..., :wide]
        sums = sums + (got[..., wide : wide + room] + got[..., wide + room :])
        reach, hop = reach * 2, hop + 1
    return states, sums


def tie(*values):
    return lax.optimization_barrier(values)


def ring_form(latents, proj_weight):
    frame_count, band_rows, column_count, channels = latents.shape
    rows = proj_weight.shape[0]
    third, shared, spare = split_rows(rows)
    common_rows = shared + 2 * spare
    count, groups = lax.axis_size("tm"), lax.axis_size("groups")
    heads_here = HEADS // 2
    tokens = frame_count * band_rows * column_count
    block = 960 if tokens % 960 == 0 else tokens
    small = 240 if tokens % 240 == 0 else tokens

    forward, backward = ring_steps(count)
    across, over = swap_pairs(groups), swap_pairs(2)
    last = count // 2

    def ring(value, up):
        return lax.ppermute(value, "tm", forward if up else backward)

    def plane_swap(up, down):
        value = jnp.concatenate([up[:third], down[common_rows:]], axis=0)
        return lax.ppermute(value, "groups", across)

    def core_swap(value):
        return lax.ppermute(value, "space", over)

    here = jnp.asarray(slot_table(count))[lax.axis_index("tm")]
    plane = lax.rem(lax.axis_index("groups"), 2)
    meta = jnp.concatenate([jnp.stack([plane, lax.axis_index("space")]), here]).astype(jnp.int32)

    up, down = pack_first(meta, proj_weight, heads_here)
    mine, theirs = pack_rest(meta, proj_weight, up)
    x = pack_tokens(latents.reshape(tokens, channels), mine, rows, count, small)

    ways = [(mine, mine)]
    half = DEPTH // 2 + spare
    mid = half // 2 // 16 * 16 + 16

    def next_queries():
        if len(ways) < last:
            ways.append((ring(ways[-1][0], True), ring(ways[-1][1], False)))
        elif len(ways) == last:
            ways.append((ring(ways[-1][0][:mid], True), ring(ways[-1][1][mid:], False)))

    def with_queries(*values):
        *values, up, down = tie(*values, *ways[-1])
        ways[-1] = up, down
        next_queries()
        return values

    def plan(bands_in, which, of_keys, has_acc, with_rest):
        return (bands_in, tuple(which), count, rows, of_keys, has_acc, with_rest, block)

    kv_shape = jax.ShapeDtypeStruct((2 * tokens, 2 * heads_here * HEAD), F32)

    def add_keys_values(acc, which):
        pieces = [part for s in which for part in slots[s]]
        settings = plan(2, which, True, acc is not None, False)
        return project(meta, both, acc, pieces, [], settings, keep, kv_shape, "kv_part")

    def thirds(up, down, up_other, down_other):
        common_up, common_down = [(up, third, common_rows)], [(down, 0, common_rows)]
        return [
            [[(up, 0, third)], [up_other], common_up],
            [[down_other], [(down, common_rows, third)], common_down],
        ]

    slots = thirds(up, down, (down, common_rows, third), (up, 0, third))[:1]
    some = common_rows // 2 // 16 * 16
    swapped, acc = None, None
    for step in range(1, last + 1):
        before = up, down
        full = step < last
        up = ring(up if full else up[: third + some], True)
        down = ring(down if full else down[some:], False)
        if step == 1:
            x = tie(x, up, down)[0]
            x_other = core_swap(x)
            both = (x, x_other)
        elif step + 1 < last:
            x_other, up, down, swapped = tie(x_other, up, down, swapped)
            both = (x, x_other)
        elif full:
            next_queries()
            acc = add_keys_values(None, range(len(slots)))
            _, up, down, swapped = tie(acc, up, down, swapped)
        else:
            acc, *ways[-1] = tie(acc, *ways[-1])
            acc = add_keys_values(acc, range(len(slots) - 2, len(slots)))
            acc, up, down, swapped = tie(acc, up, down, swapped)
            next_queries()
        if step > 1:
            slots += thirds(*before, (swapped, 0, third), (swapped, third, third))
        if full:
            swapped = plane_swap(up, down)
    rest = common_rows - some
    slots.append([[(up, 0, third)], [(down, rest, third)], [(up, third, some), (down, 0, rest)]])
    settings = plan(2, range(count - 3, count), True, True, True)
    pieces = [piece for slot in slots[count - 3 :] for piece in slot]
    commons = [slot[2] for slot in slots]
    payload = block_states(meta, both, acc, pieces, commons, settings, heads_here)
    (payload,) = with_queries(payload)

    found = [[[(mine, 0, half)], [(theirs, 0, half)]]]
    cut = 1 + 2 * ((count - 1) // 4 + (count > 4))

    def query_slots(step):
        if step < last:
            for value in ways[step]:
                found.append([[(value, 0, half)], [(core_swap(value), 0, half)]])
        else:
            value = jnp.concatenate(ways[step], axis=0)
            found.append([[(value, 0, half)], [(core_swap(value), 0, half)]])

    def project_queries(acc, which, finish, dtype, name):
        ends = which[-1] == count - 1
        pieces = [part for s in which for part in found[s]]
        every = [part for s in found for part in s] if ends else []
        settings = plan(1, which, False, acc is not None, ends)
        out = jax.ShapeDtypeStruct((tokens, HEADS * HEAD), dtype)
        return project(meta, (x,), acc, pieces, every, settings, finish, out, name)

    held = {}

    def alongside(hop, got):
        if hop == 0:
            query_slots(1)
            query_slots(2)
            (got,) = with_queries(got)
        if hop == 1:
            early = project_queries(None, range(cut), keep, F32, "q_early")
            query_slots(3)
            got, held["q"] = tie(got, early)
        if hop == 2:
            query_slots(4)
            late = project_queries(held["q"], range(cut, count), keep_features, BF, "q_late")
            got, held["q"] = tie(got, late)
        return got

    states, sums = payload[:, :HEAD], payload[:, HEAD : HEAD + 8]
    total = jnp.concatenate([*running_total(states, sums, count, alongside), sums], axis=1)
    out = attend(meta, held["q"], total, core_swap(total), heads_here, small)
    return out.reshape(frame_count, band_rows, column_count, HEADS * HEAD)


def gathered_form(latents, proj_weight):
    frame_count, band_rows, column_count, channels = latents.shape
    shard_rows = proj_weight.shape[0]
    band_count, band = lax.axis_size("space"), lax.axis_index("space")
    heads_here = HEADS // band_count
    own = proj_weight.reshape(shard_rows, 3, band_count, heads_here * HEAD)
    own = lax.dynamic_index_in_dim(own, band, 2, keepdims=False)
    own = own.reshape(shard_rows, 3 * heads_here * HEAD)
    weight = lax.all_gather(own, "tm", axis=0, tiled=True)
    tokens = lax.all_gather(latents, "space", axis=1, tiled=True)
    joined = tokens.shape[1]
    projected = dot(tokens.reshape(-1, channels), weight).astype(BF)
    split = projected.reshape(-1, 3, heads_here, HEAD)
    queries, feats, values = jax.nn.relu(split[:, 0]), jax.nn.relu(split[:, 1]), split[:, 2]
    states = jnp.einsum("nhe,nhf->hef", feats, values, preferred_element_type=F32)
    key_sums = jnp.sum(feats, axis=0, dtype=F32)
    states, key_sums = running_total(states, key_sums[:, :, None], lax.axis_size("tm"))
    states, key_sums = states.astype(BF), key_sums[:, :, 0]
    numerator = jnp.einsum("nhe,hef->nhf", queries, states, preferred_element_type=F32)
    denominator = jnp.einsum(
        "nhe,he->nh", queries.astype(F32), key_sums, precision=lax.Precision.HIGHEST
    )
    out = (numerator / (denominator[:, :, None] + 1.0)).astype(BF)
    out = out.reshape(frame_count, joined, column_count, heads_here * HEAD)
    return lax.all_to_all(out, "space", split_axis=1, concat_axis=3, tiled=True)


def on_device(latents, proj_weight):
    even = lax.axis_size("groups") % 2 == 0 and lax.axis_size("space") == 2
    if even and proj_weight.shape[0] // DEPTH == 1 and lax.axis_size("tm") == 8:
        return ring_form(latents, proj_weight)
    return gathered_form(latents, proj_weight)


def solution(mesh):
    return jax.shard_map(
        on_device,
        mesh=mesh,
        in_specs=(P(("groups", "tm"), "space", None, None), P("tm", None)),
        out_specs=P(("groups", "tm"), "space", None, None),
        check_vma=False,
    )
```

```python
import functools

import jax
import jax.numpy as jnp
import numpy as np
from jax import lax
from jax.experimental import pallas as pl
from jax.experimental.pallas import tpu as pltpu
from jax.sharding import PartitionSpec as P

HEADS = 10
HEAD = 112
LANES = 128
DEPTH = 256
BF = jnp.bfloat16
F32 = jnp.float32
LIMIT = 16 * 1024 * 1024


def ceil_to(value, step):
    return -(-value // step) * step


def dot(a, b):
    return jnp.dot(a, b, preferred_element_type=F32)


def params():
    return pltpu.CompilerParams(vmem_limit_bytes=LIMIT, dimension_semantics=("arbitrary",))


def cost(flops, moved):
    return pl.CostEstimate(flops=int(flops), bytes_accessed=int(moved), transcendentals=0)


def whole(shape):
    return pl.BlockSpec(shape, lambda i, *_: (0,) * len(shape))


def ring_order(count):
    if count % 2:
        return list(range(count))
    return list(range(0, count, 2)) + list(range(count - 1, 0, -2))


def slot_table(count):
    order = ring_order(count)
    up, down = count // 2, (count - 1) // 2
    table = np.zeros((count, count), np.int32)
    for at, index in enumerate(order):
        slots = [0]
        for step in range(1, up + 1):
            slots.append(-step)
            if step <= down:
                slots.append(step)
        table[index] = [order[(at + s) % count] for s in slots]
    return table


def split_rows(rows):
    third = ceil_to(DEPTH // 3, 16)
    spare = ceil_to((rows - DEPTH + 1) // 2, 16)
    return third, DEPTH - 2 * third, spare


def resident(kernel, meta, operands, outs, scratch, flops, name, aliases=None):
    in_vmem = pl.BlockSpec(memory_space=pltpu.VMEM)
    return pl.pallas_call(
        kernel,
        in_specs=[pl.BlockSpec(memory_space=pltpu.SMEM)] + [in_vmem] * len(operands),
        out_specs=[in_vmem] * len(outs),
        out_shape=outs,
        scratch_shapes=scratch,
        input_output_aliases=aliases or {},
        compiler_params=pltpu.CompilerParams(vmem_limit_bytes=LIMIT),
        cost_estimate=cost(flops, 0),
        name=name,
    )(meta, *operands)


def key_value_columns(meta, heads_here, run):
    wide, model = heads_here * HEAD, HEADS * HEAD

    def on_core(core):
        for part in (1, 2):
            begin = part * model + core * wide
            run(slice(begin, begin + wide), slice((part - 1) * wide, part * wide))

    for core in range(HEADS // heads_here):
        pl.when(meta[1] == core)(functools.partial(on_core, core))


def pack_first_kernel(meta, w_ref, up_ref, down_ref, *, heads_here):
    rows = w_ref.shape[0]
    third, shared, spare = split_rows(rows)
    own, other = (pl.ds(pl.multiple_of(p * third, 16), third) for p in (meta[0], 1 - meta[0]))
    end = up_ref.shape[0]
    blank = 2 * spare - (rows - DEPTH)
    common = shared + 2 * spare
    for ref, at in ((up_ref, end - blank), (down_ref, common - blank)):
        ref[at : at + blank, :] = jnp.zeros((blank, ref.shape[1]), BF)

    def run(of, to):
        for ref, take, at, common_at in ((up_ref, own, 0, third), (down_ref, other, common, 0)):
            ref[at : at + third, to] = w_ref[take, of]
            ref[common_at : common_at + common - blank, to] = w_ref[2 * third :, of]

    key_value_columns(meta, heads_here, run)


def pack_rest_kernel(meta, w_ref, after_ref, mine_ref, theirs_ref):
    rows = w_ref.shape[0]
    spare = split_rows(rows)[2]
    half, model = DEPTH // 2, HEADS * HEAD

    def queries(out_ref, core):
        out_ref[:half, :] = w_ref[core * half : (core + 1) * half, :model]
        out_ref[half:, :] = jnp.zeros((spare, model), BF)
        begin = DEPTH + core * spare
        count = min(spare, rows - begin)
        out_ref[half : half + count, :] = w_ref[begin : begin + count, :model]

    for core in range(2):
        pl.when(meta[1] == core)(functools.partial(queries, mine_ref, core))
        pl.when(meta[1] == 1 - core)(functools.partial(queries, theirs_ref, core))


def pack_first(meta, w, heads_here):
    third, shared, spare = split_rows(w.shape[0])
    out = jax.ShapeDtypeStruct((third + shared + 2 * spare, 2 * heads_here * HEAD), BF)
    kernel = functools.partial(pack_first_kernel, heads_here=heads_here)
    return resident(kernel, meta, [w], [out] * 2, [], 1e9, "pack_first")


def pack_rest(meta, w, after):
    half = DEPTH // 2 + split_rows(w.shape[0])[2]
    outs = [jax.ShapeDtypeStruct((half, HEADS * HEAD), BF)] * 2
    return resident(pack_rest_kernel, meta, [w, after], outs, [], 1e9, "pack_rest")


def pack_tokens_kernel(x_ref, after_ref, o_ref, *, rows, count):
    spare = split_rows(rows)[2]
    rest = rows - DEPTH
    blank = jnp.zeros((x_ref.shape[0], 2 * spare - rest), x_ref.dtype)
    left_over = []
    for j in range(count):
        at = j * rows
        o_ref[:, j * DEPTH : (j + 1) * DEPTH] = x_ref[:, at : at + DEPTH]
        left_over += [x_ref[:, at + DEPTH : at + rows], blank]
    o_ref[:, count * DEPTH :] = jnp.concatenate(left_over, axis=1)


def pack_tokens(x, after, rows, count, block):
    tokens, channels = x.shape
    depth = count * (DEPTH + 2 * split_rows(rows)[2])
    return pl.pallas_call(
        functools.partial(pack_tokens_kernel, rows=rows, count=count),
        grid=(tokens // block,),
        in_specs=[
            pl.BlockSpec((block, channels), lambda i: (i, 0)),
            pl.BlockSpec(memory_space=pl.ANY),
        ],
        out_specs=pl.BlockSpec((block, depth), lambda i: (i, 0)),
        out_shape=jax.ShapeDtypeStruct((tokens, depth), BF),
        compiler_params=params(),
        cost_estimate=cost(0, 4 * x.size),
        name="pack_tokens",
    )(x, after)


def put(weights, at, step, value):
    weights[pl.ds(pl.multiple_of(at, step), value.shape[0]), :] = value


def put_rows(weights, at, piece, begin, end):
    offset = 0
    for ref, first, count in piece:
        low, high = max(begin, offset), min(end, offset + count)
        if low < high:
            put(weights, at + low - begin, 16, ref[first + low - offset : first + high - offset, :])
        offset += count


def fill_keys_values(weights, meta, slots, pieces, rows):
    third, shared, _ = split_rows(rows)
    for s in range(len(slots)):
        own, other, common = pieces[3 * s : 3 * s + 3]
        put_rows(weights, s * DEPTH + meta[0] * third, own, 0, third)
        put_rows(weights, s * DEPTH + (1 - meta[0]) * third, other, 0, third)
        put_rows(weights, s * DEPTH + 2 * third, common, 0, shared)


def fill_queries(weights, meta, slots, pieces, rows):
    half = DEPTH // 2
    for s in range(len(slots)):
        for piece, core in zip(pieces[2 * s : 2 * s + 2], (meta[1], 1 - meta[1])):
            put_rows(weights, s * DEPTH + core * half, piece, 0, half)


def fill_left_over(weights, meta, base, pieces, rows, of_keys):
    third, shared, spare = split_rows(rows)
    if of_keys:
        for s, piece in enumerate(pieces):
            at = base + meta[2 + s] * 2 * spare
            put_rows(weights, at, piece, shared, shared + 2 * spare)
        return
    half = DEPTH // 2
    for s in range(len(pieces) // 2):
        for piece, core in zip(pieces[2 * s : 2 * s + 2], (meta[1], 1 - meta[1])):
            put_rows(weights, base + (meta[2 + s] * 2 + core) * spare, piece, half, half + spare)


def token_columns(x_ref, rows, meta, slots, count, with_rest):
    taken = [x_ref[rows, pl.ds(pl.multiple_of(meta[2 + s] * DEPTH, DEPTH), DEPTH)] for s in slots]
    if with_rest:
        taken.append(x_ref[rows, count * DEPTH :])
    return jnp.concatenate(taken, axis=1)


def every_block(xs, block, run):
    tokens = xs[0].shape[0]
    for band, x_ref in enumerate(xs):

        def step(i, carry, band=band, x_ref=x_ref):
            at = pl.multiple_of(i * block, block)
            run(x_ref, pl.ds(at, block), pl.ds(pl.multiple_of(at + band * tokens, block), block))
            return carry

        lax.fori_loop(0, tokens // block, step, 0)


def project_kernel(meta, *refs, plan, where, finish):
    bands_in, slots, count, rows, of_keys, has_acc, with_rest, block = plan
    xs, refs = refs[:bands_in], refs[bands_in:]
    acc_ref, refs = (refs[0], refs[1:]) if has_acc else (None, refs)
    pieces, rest_pieces = (
        [[(refs[i], at, n) for i, at, n in piece] for piece in pieces] for pieces in where
    )
    refs = refs[1 + max(i for pieces in where for piece in pieces for i, _, _ in piece) :]
    weights, refs = refs[-1], refs[:-1]
    (fill_keys_values if of_keys else fill_queries)(weights, meta, slots, pieces, rows)
    if with_rest:
        fill_left_over(weights, meta, len(slots) * DEPTH, rest_pieces, rows, of_keys)

    def run(x_ref, rows_here, rows_of_all):
        x = token_columns(x_ref, rows_here, meta, slots, count, with_rest)
        total = dot(x, weights[...])
        if has_acc:
            total = total + acc_ref[rows_of_all, :]
        finish(refs, total, rows_of_all)

    every_block(xs, block, run)


def keep(refs, total, rows):
    refs[0][rows, :] = total


def keep_features(refs, total, rows):
    refs[0][rows, :] = jnp.maximum(total.astype(BF), 0)


def distinct(*lists):
    arrays, places = [], {}
    for array, _, _ in (part for pieces in lists for piece in pieces for part in piece):
        if id(array) not in places:
            places[id(array)] = len(arrays)
            arrays.append(array)
    where = tuple(
        tuple(tuple((places[id(a)], at, n) for a, at, n in piece) for piece in pieces)
        for pieces in lists
    )
    return arrays, where


def project(meta, xs, acc, pieces, rest_pieces, plan, finish, out, name):
    bands_in, slots, count, rows, of_keys, has_acc, with_rest, block = plan
    arrays, where = distinct(pieces, rest_pieces)
    wide = arrays[0].shape[1]
    depth = len(slots) * DEPTH + with_rest * count * 2 * split_rows(rows)[2]
    tokens = bands_in * xs[0].shape[0]
    operands = [*xs, *([acc] if has_acc else []), *arrays]
    in_place = has_acc and out.shape == acc.shape and out.dtype == acc.dtype
    return resident(
        functools.partial(project_kernel, plan=plan, where=where, finish=finish),
        meta,
        operands,
        [out],
        [pltpu.VMEM((depth, wide), BF)],
        2 * tokens * depth * wide,
        name,
        {1 + bands_in: 0} if in_place else None,
    )[0]


def states_kernel(meta, *refs, plan, where, heads_here):
    out_ref, values, weights = refs[-3:]
    wide = heads_here * HEAD
    values[...] = jnp.ones_like(values)
    out_ref[...] = jnp.zeros_like(out_ref)

    def finish(_, projected, rows):
        projected = projected.astype(BF)
        feats = jnp.maximum(projected[:, :wide], 0).T
        for h in range(heads_here):
            rows = slice(h * HEAD, (h + 1) * HEAD)
            values[:, :HEAD] = projected[:, wide + h * HEAD : wide + (h + 1) * HEAD]
            out_ref[rows, :] += dot(feats[rows, :], values[...])

    project_kernel(meta, *refs, plan=plan, where=where, finish=finish)


def block_states(meta, xs, acc, pieces, rest_pieces, plan, heads_here):
    wide = heads_here * HEAD
    bands_in, slots, count, rows, _, has_acc, with_rest, block = plan
    depth = len(slots) * DEPTH + with_rest * count * 2 * split_rows(rows)[2]
    tokens = bands_in * xs[0].shape[0]
    arrays, where = distinct(pieces, rest_pieces)
    return resident(
        functools.partial(states_kernel, plan=plan, where=where, heads_here=heads_here),
        meta,
        [*xs, acc, *arrays],
        [jax.ShapeDtypeStruct((wide, LANES), F32)],
        [
            pltpu.VMEM((block, LANES), BF),
            pltpu.VMEM((depth, 2 * wide), BF),
        ],
        2 * tokens * (depth * 2 * wide + wide * LANES),
        "states",
    )[0]


def bands():
    model = HEADS * HEAD
    found = []
    for left in range(0, model, 256):
        right = min(left + 256, model)
        heads = range(left // HEAD, -(-right // HEAD))
        low = heads[0] * HEAD // LANES * LANES
        high = min(ceil_to((heads[-1] + 1) * HEAD, LANES), model)
        found.append((left, right, low, high, heads))
    return found


def attend_kernel(
    meta, q_ref, mine_ref, theirs_ref, out_hbm, states, sums, held, sems, *, heads_here
):
    states[...] = jnp.zeros_like(states)
    mine, theirs = mine_ref[...], theirs_ref[...]
    parts = [jnp.where(meta[1] == k, mine, theirs) for k in range(HEADS // heads_here)]
    base = 0
    for left, right, low, high, heads in bands():
        for h in heads:
            at = (h % heads_here) * HEAD
            begin, end = max(h * HEAD, left), min((h + 1) * HEAD, right)
            rows = slice(base + h * HEAD - low, base + (h + 1) * HEAD - low)
            block = parts[h // heads_here][at : at + HEAD, begin - h * HEAD : end - h * HEAD]
            states[rows, begin - left : end - left] = block.astype(BF)
        base += high - low
    lane = lax.broadcasted_iota(jnp.int32, (HEAD, LANES), 1)
    for h in range(HEADS):
        at = (h % heads_here) * HEAD
        key_sums = parts[h // heads_here][at : at + HEAD, HEAD : HEAD + 1]
        key_sums = jnp.broadcast_to(key_sums, (HEAD, LANES))
        upper = key_sums.astype(BF).astype(F32)
        chosen = jnp.where(lane == h, upper, jnp.where(lane == h + 64, key_sums - upper, 0.0))
        sums[h * HEAD : (h + 1) * HEAD, :] = chosen.astype(BF)
    blocks, block = held.shape[0], held.shape[1]
    column = lax.broadcasted_iota(jnp.int32, (block, LANES), 1)
    shares = []
    for i in range(blocks):
        total = dot(q_ref[i * block : (i + 1) * block, :], sums[...])
        shares.append(1.0 / (total + pltpu.roll(total, 64, 1) + 1.0))

    def send(i):
        return pltpu.make_async_copy(held.at[i], out_hbm.at[pl.ds(i * block, block)], sems.at[i])

    for i in range(blocks):
        base = 0
        for left, right, low, high, _ in bands():
            q = q_ref[i * block : (i + 1) * block, low:high]
            numerator = dot(q, states[base : base + high - low, :])
            for at in range(left, right, LANES):
                width = min(LANES, right - at)
                head = sum((column + at >= h * HEAD).astype(jnp.int32) for h in range(1, HEADS))
                scale = jnp.take_along_axis(shares[i], head, axis=1)
                scaled = (numerator[:, at - left : at - left + LANES] * scale).astype(BF)
                held[i, :, at : at + width] = scaled[:, :width]
            base += high - low
        send(i).start()
    for i in range(blocks):
        send(i).wait()


def attend(meta, queries, mine, theirs, heads_here, block):
    tokens, model = queries.shape
    rows = sum(high - low for _, _, low, high, _ in bands())
    in_vmem = pl.BlockSpec(memory_space=pltpu.VMEM)
    return pl.pallas_call(
        functools.partial(attend_kernel, heads_here=heads_here),
        in_specs=[pl.BlockSpec(memory_space=pltpu.SMEM)] + [in_vmem] * 3,
        out_specs=pl.BlockSpec(memory_space=pl.ANY),
        scratch_shapes=[
            pltpu.VMEM((rows, 256), BF),
            pltpu.VMEM((model, LANES), BF),
            pltpu.VMEM((tokens // block, block, model), BF),
            pltpu.SemaphoreType.DMA((tokens // block,)),
        ],
        out_shape=jax.ShapeDtypeStruct((tokens, model), BF),
        compiler_params=pltpu.CompilerParams(vmem_limit_bytes=LIMIT),
        cost_estimate=cost(2 * tokens * model * 800, tokens * model * 4),
        name="attend",
    )(meta, queries, mine, theirs)


def swap_pairs(count):
    return [(i, i ^ 1) for i in range(count)]


def ring_steps(count):
    order = ring_order(count)
    forward = [(order[i], order[(i + 1) % count]) for i in range(count)]
    return forward, [(b, a) for a, b in forward]


def running_total(states, sums, count, alongside=None):
    wide, room = states.shape[-1], sums.shape[-1]
    hops = []

    def send(values, pairs):
        states, sums = values
        upper = sums.astype(BF)
        lower = (sums - upper.astype(F32)).astype(BF)
        got = lax.ppermute(jnp.concatenate([states.astype(BF), upper, lower], axis=-1), "tm", pairs)
        if alongside is not None:
            got = alongside(len(hops), got)
        hops.append(got)
        got = got.astype(F32)
        return got[..., :wide], got[..., wide : wide + room] + got[..., wide + room :]

    def add(one, two):
        return one[0] + two[0], one[1] + two[1]

    window, total = (states, sums), (states, sums)
    stride = 1
    if count % 2 == 0:
        stride = 2
        partner = send(window, swap_pairs(count))
        window = add(window, partner)
        second = lax.rem(lax.axis_index("tm"), 2) == 1
        total = tuple(jnp.where(second, both, own) for both, own in zip(window, total))
    while stride < count:
        got = send(window, [(i, i + stride) for i in range(count - stride)])
        total, window = add(total, got), add(window, got)
        stride *= 2
    return total


def tie(*values):
    return lax.optimization_barrier(values)


def ring_form(latents, proj_weight):
    frame_count, band_rows, column_count, channels = latents.shape
    rows = proj_weight.shape[0]
    third, shared, spare = split_rows(rows)
    common_rows = shared + 2 * spare
    count, groups = lax.axis_size("tm"), lax.axis_size("groups")
    heads_here = HEADS // 2
    tokens = frame_count * band_rows * column_count
    block = 960 if tokens % 960 == 0 else tokens
    small = 240 if tokens % 240 == 0 else tokens

    forward, backward = ring_steps(count)
    across, over = swap_pairs(groups), swap_pairs(2)
    last = count // 2

    def ring(value, up):
        return lax.ppermute(value, "tm", forward if up else backward)

    def plane_swap(up, down):
        value = jnp.concatenate([up[:third], down[common_rows:]], axis=0)
        return lax.ppermute(value, "groups", across)

    def core_swap(value):
        return lax.ppermute(value, "space", over)

    here = jnp.asarray(slot_table(count))[lax.axis_index("tm")]
    plane = lax.rem(lax.axis_index("groups"), 2)
    meta = jnp.concatenate([jnp.stack([plane, lax.axis_index("space")]), here]).astype(jnp.int32)

    up, down = pack_first(meta, proj_weight, heads_here)
    mine, theirs = pack_rest(meta, proj_weight, up)
    x = pack_tokens(latents.reshape(tokens, channels), mine, rows, count, small)

    ways = [(mine, mine)]
    half = DEPTH // 2 + spare
    mid = half // 2 // 16 * 16 + 16

    def next_queries():
        if len(ways) < last:
            ways.append((ring(ways[-1][0], True), ring(ways[-1][1], False)))
        elif len(ways) == last:
            ways.append((ring(ways[-1][0][:mid], True), ring(ways[-1][1][mid:], False)))

    def with_queries(*values):
        *values, up, down = tie(*values, *ways[-1])
        ways[-1] = up, down
        next_queries()
        return values

    def plan(bands_in, which, of_keys, has_acc, with_rest):
        return (bands_in, tuple(which), count, rows, of_keys, has_acc, with_rest, block)

    kv_shape = jax.ShapeDtypeStruct((2 * tokens, 2 * heads_here * HEAD), F32)

    def add_keys_values(acc, which):
        pieces = [part for s in which for part in slots[s]]
        settings = plan(2, which, True, acc is not None, False)
        return project(meta, both, acc, pieces, [], settings, keep, kv_shape, "kv_part")

    def thirds(up, down, up_other, down_other):
        common_up, common_down = [(up, third, common_rows)], [(down, 0, common_rows)]
        return [
            [[(up, 0, third)], [up_other], common_up],
            [[down_other], [(down, common_rows, third)], common_down],
        ]

    slots = thirds(up, down, (down, common_rows, third), (up, 0, third))[:1]
    some = common_rows // 2 // 16 * 16
    swapped, acc = None, None
    for step in range(1, last + 1):
        before = up, down
        full = step < last
        up = ring(up if full else up[: third + some], True)
        down = ring(down if full else down[some:], False)
        if step == 1:
            x = tie(x, up, down)[0]
            x_other = core_swap(x)
            both = (x, x_other)
        elif step + 1 < last:
            x_other, up, down, swapped = tie(x_other, up, down, swapped)
            both = (x, x_other)
        elif full:
            next_queries()
            acc = add_keys_values(None, range(len(slots)))
            _, up, down, swapped = tie(acc, up, down, swapped)
        else:
            acc, *ways[-1] = tie(acc, *ways[-1])
            acc = add_keys_values(acc, range(len(slots) - 2, len(slots)))
            acc, up, down, swapped = tie(acc, up, down, swapped)
            next_queries()
        if step > 1:
            slots += thirds(*before, (swapped, 0, third), (swapped, third, third))
        if full:
            swapped = plane_swap(up, down)
    rest = common_rows - some
    slots.append([[(up, 0, third)], [(down, rest, third)], [(up, third, some), (down, 0, rest)]])
    settings = plan(2, range(count - 3, count), True, True, True)
    pieces = [piece for slot in slots[count - 3 :] for piece in slot]
    commons = [slot[2] for slot in slots]
    payload = block_states(meta, both, acc, pieces, commons, settings, heads_here)
    (payload,) = with_queries(payload)

    found = [[[(mine, 0, half)], [(theirs, 0, half)]]]
    cut = 1 + 2 * ((count - 1) // 4 + (count > 4))

    def query_slots(step):
        if step < last:
            for value in ways[step]:
                found.append([[(value, 0, half)], [(core_swap(value), 0, half)]])
        else:
            value = jnp.concatenate(ways[step], axis=0)
            found.append([[(value, 0, half)], [(core_swap(value), 0, half)]])

    def project_queries(acc, which, finish, dtype, name):
        ends = which[-1] == count - 1
        pieces = [part for s in which for part in found[s]]
        every = [part for s in found for part in s] if ends else []
        settings = plan(1, which, False, acc is not None, ends)
        out = jax.ShapeDtypeStruct((tokens, HEADS * HEAD), dtype)
        return project(meta, (x,), acc, pieces, every, settings, finish, out, name)

    held = {}

    def alongside(hop, got):
        if hop == 0:
            query_slots(1)
            query_slots(2)
            (got,) = with_queries(got)
        if hop == 1:
            early = project_queries(None, range(cut), keep, F32, "q_early")
            query_slots(3)
            got, held["q"] = tie(got, early)
        if hop == 2:
            query_slots(4)
            late = project_queries(held["q"], range(cut, count), keep_features, BF, "q_late")
            got, held["q"] = tie(got, late)
        return got

    states, sums = payload[:, :HEAD], payload[:, HEAD : HEAD + 8]
    total = jnp.concatenate([*running_total(states, sums, count, alongside), sums], axis=1)
    out = attend(meta, held["q"], total, core_swap(total), heads_here, small)
    return out.reshape(frame_count, band_rows, column_count, HEADS * HEAD)


def gathered_form(latents, proj_weight):
    frame_count, band_rows, column_count, channels = latents.shape
    shard_rows = proj_weight.shape[0]
    band_count, band = lax.axis_size("space"), lax.axis_index("space")
    heads_here = HEADS // band_count
    own = proj_weight.reshape(shard_rows, 3, band_count, heads_here * HEAD)
    own = lax.dynamic_index_in_dim(own, band, 2, keepdims=False)
    own = own.reshape(shard_rows, 3 * heads_here * HEAD)
    weight = lax.all_gather(own, "tm", axis=0, tiled=True)
    tokens = lax.all_gather(latents, "space", axis=1, tiled=True)
    joined = tokens.shape[1]
    projected = dot(tokens.reshape(-1, channels), weight).astype(BF)
    split = projected.reshape(-1, 3, heads_here, HEAD)
    queries, feats, values = jax.nn.relu(split[:, 0]), jax.nn.relu(split[:, 1]), split[:, 2]
    states = jnp.einsum("nhe,nhf->hef", feats, values, preferred_element_type=F32)
    key_sums = jnp.sum(feats, axis=0, dtype=F32)
    states, key_sums = running_total(states, key_sums[:, :, None], lax.axis_size("tm"))
    states, key_sums = states.astype(BF), key_sums[:, :, 0]
    numerator = jnp.einsum("nhe,hef->nhf", queries, states, preferred_element_type=F32)
    denominator = jnp.einsum(
        "nhe,he->nh", queries.astype(F32), key_sums, precision=lax.Precision.HIGHEST
    )
    out = (numerator / (denominator[:, :, None] + 1.0)).astype(BF)
    out = out.reshape(frame_count, joined, column_count, heads_here * HEAD)
    return lax.all_to_all(out, "space", split_axis=1, concat_axis=3, tiled=True)


def on_device(latents, proj_weight):
    even = lax.axis_size("groups") % 2 == 0 and lax.axis_size("space") == 2
    if even and proj_weight.shape[0] // DEPTH == 1 and lax.axis_size("tm") == 8:
        return ring_form(latents, proj_weight)
    return gathered_form(latents, proj_weight)


def solution(mesh):
    return jax.shard_map(
        on_device,
        mesh=mesh,
        in_specs=(P(("groups", "tm"), "space", None, None), P("tm", None)),
        out_specs=P(("groups", "tm"), "space", None, None),
        check_vma=False,
    )
```
